256 devices in a mesh: win: 64 (over z_hi, y, x), chan: 4 (over z_lo, core).
Axes of the slice: x: 4, y: 4, z: 8 (z_hi: 4, z_lo: 2; z = z_hi * 2 + z_lo), core: 2. Of those that a mesh axis runs over, the one named last changes fastest.
Arguments:
- records: float32 [1024, 2048, 256], P('win', 'chan'), may hold values from -6 to 6
- keep: int32 [1024], P('win'), may hold values 0 or 1
- pairs: int32 [4, 2], replicated, may hold values from 0 to 15
Outputs:
- correlations: float32 [4, 16384, 512], P('chan', 'win')
The draws below stay inside these ranges and needn't reach their ends.
All inputs are finite; a program needn't handle non-finite values. No bound on the sum of `keep` on one device may be relied on, other than what follows from the above.
Results may differ from the reference program's by a relative error of at most 0.0075.
Values may be sent and summed in bfloat16 or wider, within the bound.
No kernel may reach another device: no remote copies, remote signals or barrier semaphores. Data moves between devices by JAX's collectives and lax.ppermute only.
A program may use at most 128 MiB of HBM per device.

```python
import math
import jax
import jax.numpy as jnp
from jax import lax

CH = 2048
BLK = 128
NBAND = 128
SEG = 256
NBLK = 16
SEGS_TOTAL = 1024
NPAIR = 4


def place_ends(result, stream_key, low, high):
    index_at = [jax.random.randint(jax.random.fold_in(stream_key, axis), (), 0, length) for axis, length in enumerate(result.shape)]
    longest = result.shape.index(max(result.shape))
    neighbour = index_at[:longest] + [(index_at[longest] + 1) % result.shape[longest]] + index_at[longest + 1:]
    return result.at[tuple(index_at)].set(low).at[tuple(neighbour)].set(high)


def shard_levels(stream_key, shape, cuts, least, largest):
    def one(position, parts):
        steps = jax.random.uniform(jax.random.fold_in(jax.random.fold_in(stream_key, 6), position), (parts,), jnp.float32, least / len(cuts), largest / len(cuts))
        return jnp.repeat(jnp.exp(steps), shape[position] // parts).reshape((-1,) + (1,) * (len(shape) - position - 1))

    loudness = one(*cuts[0])
    for cut in cuts[1:]:
        loudness = loudness * one(*cut)
    return loudness


def scatter_about(rng, dims, deviation, most, shards=(), kind=jnp.bfloat16):
    result = jax.random.normal(rng, dims, jnp.float32) * deviation
    if len(shards) > 0:
        result = shard_levels(rng, dims, shards, -0.22, 0.18) * result
    return jnp.clip(result, min=-most, max=most).astype(kind)


def setup_inputs(seed: int = 0) -> dict:
    arg_keys = jax.random.split(jax.random.key(seed), 4)
    return {
        "records": scatter_about(arg_keys[0], (SEGS_TOTAL, CH, SEG), 1.0, 6.0, ((0, 64), (1, 4)), jnp.float32),
        "keep": place_ends((jax.random.randint(arg_keys[1], (SEGS_TOTAL,), 0, 4) < 3).astype(jnp.int32), jax.random.fold_in(arg_keys[1], 1), 0, 1),
        "pairs": place_ends(jax.random.randint(arg_keys[2], (NPAIR, 2), 0, NBLK), jax.random.fold_in(arg_keys[2], 1), 0, NBLK - 1).astype(jnp.int32),
    }


def segment_taper(length):
    steps = jnp.arange(length, dtype=jnp.float32)
    return 0.5 - 0.5 * jnp.cos(2.0 * math.pi * (steps + 0.5) / length)

def forward_table(seg, nfft, nband):
    steps = jnp.arange(seg, dtype=jnp.int32)
    freqs = jnp.arange(1, nband + 1, dtype=jnp.int32)
    phase = (steps[:, None] * freqs[None, :] % nfft).astype(jnp.float32) * (2.0 * math.pi / nfft)
    scale = 1.0 / math.sqrt(seg)
    return (jnp.concatenate([jnp.cos(phase), -jnp.sin(phase)], axis=1) * scale).astype(jnp.bfloat16)

def inverse_table(nfft, nband):
    freqs = jnp.arange(1, nband + 1, dtype=jnp.int32)
    lagged = jnp.arange(nfft, dtype=jnp.int32) - nfft // 2
    phase = (freqs[:, None] * lagged[None, :] % nfft).astype(jnp.float32) * (2.0 * math.pi / nfft)
    return jnp.concatenate([jnp.cos(phase), -jnp.sin(phase)], axis=0).astype(jnp.bfloat16)

def prepare(records, keep):
    centred = records - lax.optimization_barrier(jnp.mean(records, axis=2, keepdims=True))
    power = lax.optimization_barrier(jnp.mean(centred * centred, axis=2, keepdims=True))
    weight = keep.astype(jnp.float32)[:, None, None]
    taper = segment_taper(records.shape[2])
    return (centred * lax.rsqrt(power + 1e-06) * taper * weight).astype(jnp.bfloat16)

def cross(left, right):
    half = left.shape[2] // 2
    lsplit = left.astype(jnp.float32).reshape(left.shape[0], left.shape[1], 2, half)
    rsplit = right.astype(jnp.float32).reshape(right.shape[0], right.shape[1], 2, half)
    turned = jnp.stack([lsplit[:, :, 1], -lsplit[:, :, 0]], axis=2)
    real = jnp.einsum('iscf,jscf->ijf', lsplit, rsplit)
    imag = jnp.einsum('iscf,jscf->ijf', turned, rsplit)
    return jnp.stack([real, imag], axis=2).reshape(left.shape[0] * right.shape[0], 2 * half)

def reference(records, keep, pairs):
    seg = records.shape[2]
    nfft = 2 * seg
    table = forward_table(seg, nfft, NBAND).astype(jnp.float32)
    back = inverse_table(nfft, NBAND)
    total = records.shape[0]

    def spectra_of(block):
        start = (block * BLK).astype(jnp.int32)
        piece = lax.dynamic_slice_in_dim(records, start, BLK, 1)
        prepared = prepare(piece, keep)
        return jnp.einsum('sct,tf->csf', prepared.astype(jnp.float32), table).astype(jnp.bfloat16)

    def one_pair(pair):
        left = spectra_of(pair[0])
        right = spectra_of(pair[1])
        stacked = cross(left, right).astype(jnp.bfloat16)
        return jnp.dot(stacked, back, preferred_element_type=jnp.float32) * (1.0 / math.sqrt(total * NBAND))
    return lax.map(one_pair, pairs)
```

```python
import math

import jax
import jax.numpy as jnp
import numpy as np
from jax import lax
from jax.experimental import pallas as pl
from jax.experimental.pallas import tpu as pltpu
from jax.sharding import Mesh
from jax.sharding import PartitionSpec as P

BLK = 128
NBAND = 128
SEG = 256
NFFT = 512
NPAIR = 4
ZH, YX, ZL, CORE = 4, 16, 2, 2
OWN_SEGS = 16
OWN_BLKS = 4
BINS = 2
F32, BF16 = jnp.float32, jnp.bfloat16
MIB = 1 << 20


def bins_of(half, quarter):
    first = (half * ZL + quarter) * YX * BINS
    return (1 + first + np.arange(YX * BINS)).reshape(YX, BINS)


def forward_rows(bins):
    phase = (bins.reshape(-1, 1) * np.arange(SEG)[None, :]) % NFFT
    angle = phase.astype(np.float64) * (2.0 * math.pi / NFFT)
    both = np.stack([np.cos(angle), -np.sin(angle)], axis=1)
    return (both.reshape(-1, SEG) / math.sqrt(SEG)).astype(np.float32)


def forward_tables():
    tables = []
    for zl in range(ZL):
        for core in range(CORE):
            rows = [
                forward_rows(bins_of(core ^ other_core, zl ^ other_z))
                for other_core in range(CORE)
                for other_z in range(ZL)
            ]
            tables.append(np.concatenate(rows))
    return np.stack(tables)


def inverse_rows():
    order = np.stack(
        [np.stack([bins_of(core, zl) for core in range(CORE)], axis=1) for zl in range(ZL)], axis=1
    )
    phase = (order.reshape(-1, 1) * (np.arange(NFFT)[None, :] - NFFT // 2)) % NFFT
    angle = phase.astype(np.float64) * (2.0 * math.pi / NFFT)
    both = np.stack([np.cos(angle), -np.sin(angle)], axis=1)
    return both.reshape(-1, 2 * BINS, NFFT).astype(np.float32)


def spectra_kernel(chan_ref, keep_ref, records_ref, table_ref, taper_ref, mine_ref, theirs_ref, rows_ref):
    table = table_ref[0]
    taper = taper_ref[...]
    for s in range(OWN_SEGS):
        samples = records_ref[s]
        centred = samples - jnp.mean(samples, axis=1, keepdims=True)
        power = jnp.mean(centred * centred, axis=1, keepdims=True)
        weight = keep_ref[s].astype(F32)
        prepared = (centred * lax.rsqrt(power + 1e-06) * taper * weight).astype(BF16)
        spectra = lax.dot_general(table, prepared, (((1,), (1,)), ((), ())), preferred_element_type=F32)
        rows_ref[pl.ds(s, 2 * NBAND, stride=OWN_SEGS), :] = spectra
    half = NBAND * OWN_SEGS
    shape = (ZL, 1, YX, 2 * BINS, OWN_SEGS, BLK)
    mine_ref[...] = rows_ref[:half, :].astype(BF16).reshape(shape)
    theirs_ref[...] = rows_ref[half:, :].astype(BF16).reshape(shape)


def spectra_of(records, keep, chan):
    tables = jnp.asarray(forward_tables(), BF16)
    steps = np.arange(SEG, dtype=np.float64)
    taper = jnp.asarray((0.5 - 0.5 * np.cos(2.0 * math.pi * (steps + 0.5) / SEG)).astype(np.float32)[None])
    out = jax.ShapeDtypeStruct((ZL, OWN_BLKS, YX, 2 * BINS, OWN_SEGS, BLK), BF16)
    out_spec = pl.BlockSpec((ZL, 1, YX, 2 * BINS, OWN_SEGS, BLK), lambda b, c, k: (0, b, 0, 0, 0, 0))
    return pl.pallas_call(
        spectra_kernel,
        grid_spec=pltpu.PrefetchScalarGridSpec(
            num_scalar_prefetch=2,
            grid=(OWN_BLKS,),
            in_specs=[
                pl.BlockSpec((OWN_SEGS, BLK, SEG), lambda b, c, k: (0, b, 0)),
                pl.BlockSpec((1, 2 * NBAND, SEG), lambda b, c, k: (c[0], 0, 0)),
                pl.BlockSpec((1, SEG), lambda b, c, k: (0, 0)),
            ],
            out_specs=[out_spec, out_spec],
            scratch_shapes=[pltpu.VMEM((2 * NBAND * OWN_SEGS, BLK), F32)],
        ),
        out_shape=[out, out],
        compiler_params=pltpu.CompilerParams(vmem_limit_bytes=32 * MIB),
        cost_estimate=pl.CostEstimate(flops=2 * 8192 * 256 * 256, bytes_accessed=13 * MIB, transcendentals=8192),
        name="spectra",
    )(chan, keep, records, tables, taper)


def whose(block, zl, core):
    return block // (CORE * OWN_BLKS) == zl, (block // OWN_BLKS) % CORE == core


def half_entry(ref, *at):
    return ref.at[at]


def sending_kernel(place_ref, pairs_ref, mine_ref, other_ref, inner_ref, outer_ref):
    zl, core = place_ref[0], place_ref[1]

    def take(block, bin_, d):
        _, own = whose(block, zl, core)
        slot = block % OWN_BLKS
        rows = pl.ds(bin_ * 2, 2)
        return jnp.where(own, mine_ref[1, slot, d, rows], other_ref[1, slot, d, rows])

    for p in range(NPAIR):
        a, b = pairs_ref[2 * p], pairs_ref[2 * p + 1]
        here_a, _ = whose(a, zl, core)
        here_b, _ = whose(b, zl, core)
        both = here_a & here_b
        first = jnp.where(here_a, a, b)
        second = jnp.where(both, b, first)
        second_bin = jnp.where(both, 0, 1)

        def step(d, carry, p=p, a=a, b=b, first=first, second=second, second_bin=second_bin):
            inner_ref[d, p, 0] = take(first, 0, d)
            inner_ref[d, p, 1] = take(second, second_bin, d)
            outer_ref[d, p, 0] = take(a, 1, d)
            outer_ref[d, p, 1] = take(b, 1, d)
            return carry

        lax.fori_loop(0, YX, step, 0)


def vmem():
    return pl.BlockSpec(memory_space=pltpu.VMEM)


def smem():
    return pl.BlockSpec(memory_space=pltpu.SMEM)


def sending(place, pairs, mine, other):
    out = jax.ShapeDtypeStruct((YX, NPAIR, 2, 2, OWN_SEGS, BLK), BF16)
    return pl.pallas_call(
        sending_kernel,
        in_specs=[smem(), smem(), vmem(), vmem()],
        out_specs=[vmem(), vmem()],
        out_shape=[out, out],
        compiler_params=pltpu.CompilerParams(vmem_limit_bytes=32 * MIB),
        cost_estimate=pl.CostEstimate(flops=0, bytes_accessed=4 * MIB, transcendentals=0),
        name="sending",
    )(place, pairs, mine, other)


def factors_kernel(place_ref, pairs_ref, mine_ref, other_ref, inner_ref, outer_ref, out_ref):
    zl, core = place_ref[0], place_ref[1]
    for p in range(NPAIR):
        blocks = (pairs_ref[2 * p], pairs_ref[2 * p + 1])
        here = [whose(block, zl, core)[0] for block in blocks]
        for side in range(2):
            block = blocks[side]
            own = whose(block, zl, core)[1]
            slot = block % OWN_BLKS
            lone = here[1 - side]

            def step(d, carry, p=p, side=side, own=own, slot=slot, lone=lone, is_here=here[side]):
                for bin_ in range(BINS):
                    rows = pl.ds(bin_ * 2, 2)
                    kept = jnp.where(own, mine_ref[0, slot, d, rows], other_ref[0, slot, d, rows])
                    apart = inner_ref[d, p, bin_]
                    together = inner_ref[d, p, side] if bin_ == 0 else outer_ref[d, p, side]
                    came = jnp.where(lone, apart, together)
                    out_ref[d, p, side, rows] = jnp.where(is_here, kept, came)
                return carry

            lax.fori_loop(0, YX, step, 0)


def factors(place, pairs, mine, other, inner, outer):
    return pl.pallas_call(
        factors_kernel,
        in_specs=[smem(), smem(), vmem(), vmem(), vmem(), vmem()],
        out_specs=vmem(),
        out_shape=jax.ShapeDtypeStruct((YX, NPAIR, 2, 2 * BINS, OWN_SEGS, BLK), BF16),
        compiler_params=pltpu.CompilerParams(vmem_limit_bytes=32 * MIB),
        cost_estimate=pl.CostEstimate(flops=0, bytes_accessed=6 * MIB, transcendentals=0),
        name="factors",
    )(place, pairs, mine, other, inner, outer)


def products_kernel(factors_ref, out_ref, part_ref, rows_ref):
    length = YX * OWN_SEGS
    for p in range(NPAIR):
        for bin_ in range(BINS):
            x, y = (
                jnp.concatenate(
                    [factors_ref[:, p, side, 2 * bin_ + c].reshape(length, BLK) for c in range(2)], axis=1
                )
                for side in range(2)
            )
            g = lax.dot_general(x, y, (((0,), (0,)), ((), ())), preferred_element_type=F32)
            part_ref[0] = g[:BLK, :BLK] + g[BLK:, BLK:]
            part_ref[1] = g[BLK:, :BLK] - g[:BLK, BLK:]
            for c in range(2):
                for r in range(2):
                    at = p * 8 + r * 4 + bin_ * 2 + c
                    rows_ref[pl.ds(at, BLK // 2, stride=8 * NPAIR), :] = part_ref[c, pl.ds(r, BLK // 2, stride=2), :]
    out_ref[...] = rows_ref[...].astype(BF16)


def products(gathered):
    return pl.pallas_call(
        products_kernel,
        in_specs=[vmem()],
        out_specs=vmem(),
        out_shape=jax.ShapeDtypeStruct((BLK // 2 * NPAIR * 8, BLK), BF16),
        scratch_shapes=[pltpu.VMEM((2, BLK, BLK), F32), pltpu.VMEM((BLK // 2 * NPAIR * 8, BLK), F32)],
        compiler_params=pltpu.CompilerParams(vmem_limit_bytes=32 * MIB),
        cost_estimate=pl.CostEstimate(flops=2 * 8 * 256**3, bytes_accessed=3 * MIB, transcendentals=0),
        name="products",
    )(gathered)


def lags_kernel(scale, shares_ref, back_ref, out_ref):
    total = shares_ref[0].astype(F32)
    for z in range(1, ZH):
        total += shares_ref[z].astype(F32)
    stacked = total.astype(BF16)
    for r in range(2):
        lagged = lax.dot_general(stacked, back_ref[r], (((0,), (0,)), ((), ())), preferred_element_type=F32)
        out_ref[0, r * BLK : (r + 1) * BLK, :] = lagged * scale


def lags(shares, total):
    rows = inverse_rows()
    back = np.zeros((2, rows.shape[0], 2, 2 * BINS, NFFT), np.float32)
    for r in range(2):
        back[r, :, r] = rows
    back = jnp.asarray(back.reshape(2, 4 * NBAND, NFFT), BF16)
    scale = 1.0 / math.sqrt(total * NBAND)
    return pl.pallas_call(
        lambda *refs: lags_kernel(scale, *refs),
        in_specs=[vmem(), vmem()],
        out_specs=vmem(),
        out_shape=jax.ShapeDtypeStruct((1, 2 * BLK, NFFT), F32),
        compiler_params=pltpu.CompilerParams(vmem_limit_bytes=32 * MIB),
        cost_estimate=pl.CostEstimate(flops=4 * 512 * 128 * 512, bytes_accessed=2 * MIB, transcendentals=0),
        name="lags",
    )(shares, back)


def shards(records, keep, pairs):
    zl, core = lax.axis_index("zl"), lax.axis_index("core")
    place = jnp.stack([zl, core]).astype(jnp.int32)
    chan = (zl * CORE + core).astype(jnp.int32).reshape(1)
    flat = pairs.reshape(-1)
    mine, theirs = spectra_of(records, keep, chan)
    other = lax.ppermute(theirs, "core", [(0, 1), (1, 0)])
    inner, outer = sending(place, flat, mine, other)
    inner = lax.ppermute(inner, "zl", [(0, 1), (1, 0)])
    turns = []
    for zh in range(ZH):
        turns.append((zh * ZL, (zh - 1) % ZH * ZL + 1))
        turns.append((zh * ZL + 1, (zh + 1) % ZH * ZL))
    outer = lax.ppermute(outer, ("zh", "zl"), turns)
    sides = factors(place, flat, mine, other, inner, outer)
    gathered = lax.all_to_all(sides, ("y", "x"), 0, 0, tiled=True)
    shares = products(gathered).reshape(ZH * YX * NPAIR, 8, BLK)
    shares = lax.all_to_all(shares, ("zh", "y", "x", "zl", "core"), 0, 0, tiled=True)
    total = records.shape[0] * ZH * YX
    return lags(shares.reshape(ZH, YX * NPAIR * 8, BLK), total)


def solution(mesh):
    fine = Mesh(mesh.devices.reshape(ZH, 4, 4, ZL, CORE), ("zh", "y", "x", "zl", "core"))
    win, chan = ("zh", "y", "x"), ("zl", "core")
    in_specs = (P(win, chan, None), P(win), P())
    out_specs = P(chan, win, None)
    return jax.shard_map(shards, mesh=fine, in_specs=in_specs, out_specs=out_specs, check_vma=False)
```

```python
import math

import jax
import jax.numpy as jnp
import numpy as np
from jax import lax
from jax.experimental import pallas as pl
from jax.experimental.pallas import tpu as pltpu
from jax.sharding import Mesh
from jax.sharding import PartitionSpec as P

BLK = 128
NBAND = 128
SEG = 256
NFFT = 512
NPAIR = 4
ZH, YX, ZL, CORE = 4, 16, 2, 2
OWN_SEGS = 16
OWN_BLKS = 4
BINS = 2
F32, BF16 = jnp.float32, jnp.bfloat16
MIB = 1 << 20


def bins_of(half, quarter):
    first = (half * ZL + quarter) * YX * BINS
    return (1 + first + np.arange(YX * BINS)).reshape(YX, BINS)


def forward_rows(bins):
    phase = (bins.reshape(-1, 1) * np.arange(SEG)[None, :]) % NFFT
    angle = phase.astype(np.float64) * (2.0 * math.pi / NFFT)
    both = np.stack([np.cos(angle), -np.sin(angle)], axis=1)
    return (both.reshape(-1, SEG) / math.sqrt(SEG)).astype(np.float32)


def forward_tables():
    tables = []
    for zl in range(ZL):
        for core in range(CORE):
            near = [bins_of(0, zl), bins_of(1, zl)]
            far = [bins_of(core, zl ^ 1), bins_of(core ^ 1, zl ^ 1)]
            tables.append(np.concatenate([forward_rows(bins) for bins in near + far]))
    return np.stack(tables)


def inverse_rows():
    order = np.stack(
        [np.stack([bins_of(core, zl) for core in range(CORE)], axis=1) for zl in range(ZL)], axis=1
    )
    phase = (order.reshape(-1, 1) * (np.arange(NFFT)[None, :] - NFFT // 2)) % NFFT
    angle = phase.astype(np.float64) * (2.0 * math.pi / NFFT)
    both = np.stack([np.cos(angle), -np.sin(angle)], axis=1)
    return both.reshape(-1, 2 * BINS, NFFT).astype(np.float32)


def spectra_kernel(chan_ref, keep_ref, records_ref, table_ref, taper_ref, *refs):
    outs, rows_ref = refs[:-1], refs[-1]
    table = table_ref[0]
    taper = taper_ref[...]
    for s in range(OWN_SEGS):
        samples = records_ref[s]
        centred = samples - jnp.mean(samples, axis=1, keepdims=True)
        power = jnp.mean(centred * centred, axis=1, keepdims=True)
        weight = keep_ref[s].astype(F32)
        prepared = (centred * (lax.rsqrt(power + 1e-06) * weight) * taper).astype(BF16)
        spectra = lax.dot_general(table, prepared, (((1,), (1,)), ((), ())), preferred_element_type=F32)
        rows_ref[pl.ds(s, NBAND, stride=OWN_SEGS), :] = spectra
    length = NBAND * OWN_SEGS // len(outs)
    for n, out_ref in enumerate(outs):
        part = rows_ref[n * length : (n + 1) * length, :]
        out_ref[...] = part.astype(BF16).reshape(out_ref.shape)


def in_hbm(x):
    return pltpu.with_memory_space_constraint(x, pltpu.HBM)


def spectra(half, lead, count, name, chan, keep, records, tables):
    steps = np.arange(SEG, dtype=np.float64)
    taper = jnp.asarray((0.5 - 0.5 * np.cos(2.0 * math.pi * (steps + 0.5) / SEG)).astype(np.float32)[None])
    tail = (YX, 2 * BINS, OWN_SEGS, BLK)
    out = jax.ShapeDtypeStruct(lead + (OWN_BLKS,) + tail, BF16)
    out_spec = pl.BlockSpec(lead + (1,) + tail, lambda b, *_: (0,) * len(lead) + (b, 0, 0, 0, 0))
    return pl.pallas_call(
        spectra_kernel,
        grid_spec=pltpu.PrefetchScalarGridSpec(
            num_scalar_prefetch=2,
            grid=(OWN_BLKS,),
            in_specs=[
                pl.BlockSpec((OWN_SEGS, BLK, SEG), lambda b, *_: (0, b, 0)),
                pl.BlockSpec((1, NBAND, SEG), lambda b, c, k: (c[0], half, 0)),
                pl.BlockSpec((1, SEG), lambda b, *_: (0, 0)),
            ],
            out_specs=[out_spec] * count,
            scratch_shapes=[pltpu.VMEM((NBAND * OWN_SEGS, BLK), F32)],
        ),
        out_shape=[out] * count,
        compiler_params=pltpu.CompilerParams(vmem_limit_bytes=16 * MIB),
        cost_estimate=pl.CostEstimate(flops=8192 * 256 * 256, bytes_accessed=11 * MIB, transcendentals=8192),
        name=name,
    )(chan, keep, records, tables, in_hbm(taper))


def whose(block, zl, core):
    return block // (CORE * OWN_BLKS) == zl, (block // OWN_BLKS) % CORE == core


def vmem():
    return pl.BlockSpec(memory_space=pltpu.VMEM)


def smem():
    return pl.BlockSpec(memory_space=pltpu.SMEM)


def hbm():
    return pl.BlockSpec(memory_space=pltpu.HBM)


def copy_either(first, one, two, to, sem):
    @pl.when(first)
    def _():
        pltpu.make_async_copy(one, to, sem).start()

    @pl.when(jnp.logical_not(first))
    def _():
        pltpu.make_async_copy(two, to, sem).start()


def rows_of(bin_):
    return pl.ds(bin_ * 2, 2)


def sending_kernel(place_ref, pairs_ref, mine_ref, other_ref, inner_ref, outer_ref, sems):
    zl, core = place_ref[0], place_ref[1]
    copies = []

    def take(block, bin_, to):
        own = whose(block, zl, core)[1]
        at = (block % OWN_BLKS, slice(None), rows_of(bin_))
        sem = sems.at[len(copies)]
        copy_either(own, mine_ref.at[at], other_ref.at[at], to, sem)
        copies.append(pltpu.make_async_copy(mine_ref.at[at], to, sem))

    for p in range(NPAIR):
        a, b = pairs_ref[2 * p], pairs_ref[2 * p + 1]
        here_a, here_b = whose(a, zl, core)[0], whose(b, zl, core)[0]
        both = here_a & here_b
        first = jnp.where(here_a, a, b)
        take(first, 0, inner_ref.at[:, p, 0])
        take(jnp.where(both, b, first), jnp.where(both, 0, 1), inner_ref.at[:, p, 1])
        take(a, 1, outer_ref.at[:, p, 0])
        take(b, 1, outer_ref.at[:, p, 1])
    for copy in copies:
        copy.wait()


def sending(place, pairs, mine, other):
    out = jax.ShapeDtypeStruct((YX, NPAIR, 2, 2, OWN_SEGS, BLK), BF16)
    return pl.pallas_call(
        sending_kernel,
        in_specs=[smem(), smem(), hbm(), hbm()],
        out_specs=[hbm(), hbm()],
        out_shape=[out, out],
        scratch_shapes=[pltpu.SemaphoreType.DMA((4 * NPAIR,))],
        compiler_params=pltpu.CompilerParams(vmem_limit_bytes=4 * MIB),
        cost_estimate=pl.CostEstimate(flops=0, bytes_accessed=4 * MIB, transcendentals=0),
        name="sending",
    )(place, pairs, mine, other)


def places(pairs_ref, zl, core):
    for p in range(NPAIR):
        blocks = (pairs_ref[2 * p], pairs_ref[2 * p + 1])
        here = [whose(block, zl, core)[0] for block in blocks]
        for side in range(2):
            for bin_ in range(BINS):
                number = (2 * p + side) * BINS + bin_
                yield number, p, side, bin_, blocks[side], here[side], here[1 - side]


def kept_kernel(place_ref, pairs_ref, chip_ref, out_ref, sems):
    zl, core = place_ref[0], place_ref[1]
    for start in (True, False):
        for number, p, side, bin_, block, here, _ in places(pairs_ref, zl, core):
            at = (block % (CORE * OWN_BLKS), slice(None), rows_of(bin_))
            copy = pltpu.make_async_copy(chip_ref.at[at], out_ref.at[:, p, side, rows_of(bin_)], sems.at[number])

            @pl.when(here)
            def _(start=start, copy=copy):
                if start:
                    copy.start()
                else:
                    copy.wait()


def came_kernel(place_ref, pairs_ref, inner_ref, outer_ref, kept_ref, out_ref, sems):
    zl, core = place_ref[0], place_ref[1]
    for start in (True, False):
        for number, p, side, bin_, _, here, lone in places(pairs_ref, zl, core):
            to = out_ref.at[:, p, side, rows_of(bin_)]
            sem = sems.at[number]
            together = (inner_ref if bin_ == 0 else outer_ref).at[:, p, side]

            @pl.when(jnp.logical_not(here))
            def _(start=start, lone=lone, together=together, to=to, sem=sem, p=p, bin_=bin_):
                if start:
                    copy_either(lone, inner_ref.at[:, p, bin_], together, to, sem)
                else:
                    pltpu.make_async_copy(together, to, sem).wait()


def sides_of(kernel, name, place, pairs, *arrays):
    return pl.pallas_call(
        kernel,
        in_specs=[smem(), smem()] + [hbm()] * len(arrays),
        out_specs=hbm(),
        out_shape=jax.ShapeDtypeStruct((YX, NPAIR, 2, 2 * BINS, OWN_SEGS, BLK), BF16),
        scratch_shapes=[pltpu.SemaphoreType.DMA((2 * NPAIR * BINS,))],
        input_output_aliases={4: 0} if len(arrays) == 3 else {},
        compiler_params=pltpu.CompilerParams(vmem_limit_bytes=4 * MIB),
        cost_estimate=pl.CostEstimate(flops=0, bytes_accessed=3 * MIB, transcendentals=0),
        name=name,
    )(place, pairs, *arrays)


def products_kernel(factors_ref, out_ref, part_ref, rows_ref):
    length = YX * OWN_SEGS
    for p in range(NPAIR):
        for bin_ in range(BINS):
            x, y = (
                jnp.concatenate(
                    [factors_ref[:, p, side, 2 * bin_ + c].reshape(length, BLK) for c in range(2)], axis=1
                )
                for side in range(2)
            )
            g = lax.dot_general(x, y, (((0,), (0,)), ((), ())), preferred_element_type=F32)
            part_ref[0] = g[:BLK, :BLK] + g[BLK:, BLK:]
            part_ref[1] = g[BLK:, :BLK] - g[:BLK, BLK:]
            for c in range(2):
                for r in range(2):
                    at = p * 8 + r * 4 + bin_ * 2 + c
                    rows_ref[pl.ds(at, BLK // 2, stride=8 * NPAIR), :] = part_ref[c, pl.ds(r, BLK // 2, stride=2), :]
    out_ref[...] = rows_ref[...].astype(BF16)


def products(gathered):
    return pl.pallas_call(
        products_kernel,
        in_specs=[vmem()],
        out_specs=vmem(),
        out_shape=jax.ShapeDtypeStruct((BLK // 2 * NPAIR * 8, BLK), BF16),
        scratch_shapes=[pltpu.VMEM((2, BLK, BLK), F32), pltpu.VMEM((BLK // 2 * NPAIR * 8, BLK), F32)],
        compiler_params=pltpu.CompilerParams(vmem_limit_bytes=16 * MIB),
        cost_estimate=pl.CostEstimate(flops=2 * 8 * 256**3, bytes_accessed=3 * MIB, transcendentals=0),
        name="products",
    )(gathered)


def lags_kernel(scale, shares_ref, back_ref, out_ref):
    total = shares_ref[0].astype(F32)
    for z in range(1, ZH):
        total += shares_ref[z].astype(F32)
    stacked = total.astype(BF16)
    for r in range(2):
        lagged = lax.dot_general(stacked, back_ref[r], (((0,), (0,)), ((), ())), preferred_element_type=F32)
        out_ref[0, r * BLK : (r + 1) * BLK, :] = lagged * scale


def lags(shares, total):
    rows = inverse_rows()
    back = np.zeros((2, rows.shape[0], 2, 2 * BINS, NFFT), np.float32)
    for r in range(2):
        back[r, :, r] = rows
    back = jnp.asarray(back.reshape(2, 4 * NBAND, NFFT), BF16)
    scale = 1.0 / math.sqrt(total * NBAND)
    return pl.pallas_call(
        lambda *refs: lags_kernel(scale, *refs),
        in_specs=[vmem(), vmem()],
        out_specs=vmem(),
        out_shape=jax.ShapeDtypeStruct((1, 2 * BLK, NFFT), F32),
        compiler_params=pltpu.CompilerParams(vmem_limit_bytes=16 * MIB),
        cost_estimate=pl.CostEstimate(flops=4 * 512 * 128 * 512, bytes_accessed=2 * MIB, transcendentals=0),
        name="lags",
    )(shares, back)


def swap(x, axis):
    return lax.ppermute(x, axis, [(0, 1), (1, 0)])


def swap_outer(x):
    turns = []
    for zh in range(ZH):
        turns.append((zh * ZL, (zh - 1) % ZH * ZL + 1))
        turns.append((zh * ZL + 1, (zh + 1) % ZH * ZL))
    return lax.ppermute(x, ("zh", "zl"), turns)


def shards(records, keep, pairs):
    zl, core = lax.axis_index("zl"), lax.axis_index("core")
    place = jnp.stack([zl, core]).astype(jnp.int32)
    chan = (zl * CORE + core).astype(jnp.int32).reshape(1)
    flat = pairs.reshape(-1)
    tables = in_hbm(jnp.asarray(forward_tables(), BF16))
    records = in_hbm(records)
    mine_far, theirs_far = spectra(1, (), 2, "spectra_far", chan, keep, records, tables)
    other_far = swap(theirs_far, "core")
    inner, outer = sending(place, flat, mine_far, other_far)
    later, *_ = lax.optimization_barrier((chan, inner))
    inner, outer = swap(inner, "zl"), swap_outer(outer)
    (chip,) = spectra(0, (CORE,), 1, "spectra_near", later, keep, records, tables)
    chip = lax.all_to_all(chip, "core", 0, 0, tiled=True)
    chip = chip.reshape((CORE * OWN_BLKS,) + chip.shape[2:])
    kept = sides_of(kept_kernel, "kept", place, flat, chip)
    sides = sides_of(came_kernel, "came", place, flat, inner, outer, kept)
    gathered = lax.all_to_all(sides, ("y", "x"), 0, 0, tiled=True)
    shares = products(gathered).reshape(ZH * YX * NPAIR, 8, BLK)
    shares = lax.all_to_all(shares, ("zh", "y", "x", "zl", "core"), 0, 0, tiled=True)
    total = records.shape[0] * ZH * YX
    return lags(shares.reshape(ZH, YX * NPAIR * 8, BLK), total)


def solution(mesh):
    fine = Mesh(mesh.devices.reshape(ZH, 4, 4, ZL, CORE), ("zh", "y", "x", "zl", "core"))
    win, chan = ("zh", "y", "x"), ("zl", "core")
    in_specs = (P(win, chan, None), P(win), P())
    out_specs = P(chan, win, None)
    return jax.shard_map(shards, mesh=fine, in_specs=in_specs, out_specs=out_specs, check_vma=False)
```

```python
import functools
import math

import jax
import jax.numpy as jnp
import numpy as np
from jax import lax
from jax.experimental import pallas as pl
from jax.experimental.pallas import tpu as pltpu
from jax.sharding import Mesh
from jax.sharding import PartitionSpec as P

BLK = 128
NBAND = 128
SEG = 256
NFFT = 512
NPAIR = 4
ZH, YX, ZL, CORE = 4, 16, 2, 2
OWN_SEGS = 16
OWN_BLKS = 4
BINS = 2
LEAST = 2
F32, BF16 = jnp.float32, jnp.bfloat16
MIB = 1 << 20


def bins_of(half, quarter):
    first = (half * ZL + quarter) * YX * BINS
    return (1 + first + np.arange(YX * BINS)).reshape(YX, BINS)


def forward_rows(bins):
    phase = (bins.reshape(-1, 1) * np.arange(SEG)[None, :]) % NFFT
    angle = phase.astype(np.float64) * (2.0 * math.pi / NFFT)
    both = np.stack([np.cos(angle), -np.sin(angle)], axis=1)
    return (both.reshape(-1, SEG) / math.sqrt(SEG)).astype(np.float32)


def forward_tables():
    tables = []
    for zl in range(ZL):
        for core in range(CORE):
            near = [bins_of(0, zl), bins_of(1, zl)]
            far = [bins_of(core, zl ^ 1), bins_of(core ^ 1, zl ^ 1)]
            tables.append(np.concatenate([forward_rows(bins) for bins in near + far]))
    return np.stack(tables)


def inverse_rows():
    order = np.stack(
        [np.stack([bins_of(core, zl) for core in range(CORE)], axis=1) for zl in range(ZL)], axis=1
    )
    phase = (order.reshape(-1, 1) * (np.arange(NFFT)[None, :] - NFFT // 2)) % NFFT
    angle = phase.astype(np.float64) * (2.0 * math.pi / NFFT)
    both = np.stack([np.cos(angle), -np.sin(angle)], axis=1)
    return both.reshape(-1, 2 * BINS, NFFT).astype(np.float32)


def spectra_kernel(chan_ref, keep_ref, records_ref, table_ref, taper_ref, *refs):
    outs, rows_ref = refs[:-1], refs[-1]
    table = table_ref[0]
    taper = taper_ref[...]
    for s in range(OWN_SEGS):
        samples = records_ref[s]
        centred = samples - jnp.mean(samples, axis=1, keepdims=True)
        power = jnp.mean(centred * centred, axis=1, keepdims=True)
        weight = keep_ref[s].astype(F32)
        prepared = (centred * (lax.rsqrt(power + 1e-06) * weight) * taper).astype(BF16)
        spectra = lax.dot_general(table, prepared, (((1,), (1,)), ((), ())), preferred_element_type=F32)
        rows_ref[pl.ds(s, NBAND, stride=OWN_SEGS), :] = spectra
    length = NBAND * OWN_SEGS // len(outs)
    for n, out_ref in enumerate(outs):
        part = rows_ref[n * length : (n + 1) * length, :]
        out_ref[...] = part.astype(BF16).reshape(out_ref.shape)


def in_hbm(x):
    return pltpu.with_memory_space_constraint(x, pltpu.HBM)


def spectra(half, lead, count, name, chan, keep, records, tables):
    steps = np.arange(SEG, dtype=np.float64)
    taper = jnp.asarray((0.5 - 0.5 * np.cos(2.0 * math.pi * (steps + 0.5) / SEG)).astype(np.float32)[None])
    tail = (YX, 2 * BINS, OWN_SEGS, BLK)
    out = jax.ShapeDtypeStruct(lead + (OWN_BLKS,) + tail, BF16)
    out_spec = pl.BlockSpec(lead + (1,) + tail, lambda b, *_: (0,) * len(lead) + (b, 0, 0, 0, 0))
    return pl.pallas_call(
        spectra_kernel,
        grid_spec=pltpu.PrefetchScalarGridSpec(
            num_scalar_prefetch=2,
            grid=(OWN_BLKS,),
            in_specs=[
                pl.BlockSpec((OWN_SEGS, BLK, SEG), lambda b, *_: (0, b, 0)),
                pl.BlockSpec((1, NBAND, SEG), lambda b, c, k: (c[0], half, 0)),
                pl.BlockSpec((1, SEG), lambda b, *_: (0, 0)),
            ],
            out_specs=[out_spec] * count,
            scratch_shapes=[pltpu.VMEM((NBAND * OWN_SEGS, BLK), F32)],
        ),
        out_shape=[out] * count,
        compiler_params=pltpu.CompilerParams(vmem_limit_bytes=16 * MIB),
        cost_estimate=pl.CostEstimate(flops=8192 * 256 * 256, bytes_accessed=11 * MIB, transcendentals=8192),
        name=name,
    )(chan, keep, in_hbm(records), in_hbm(tables), in_hbm(taper))


def whose(block, zl, core):
    return block // (CORE * OWN_BLKS) == zl, (block // OWN_BLKS) % CORE == core


def vmem():
    return pl.BlockSpec(memory_space=pltpu.VMEM)


def smem():
    return pl.BlockSpec(memory_space=pltpu.SMEM)


def hbm():
    return pl.BlockSpec(memory_space=pltpu.HBM)


def copy_either(first, one, two, to, sem):
    @pl.when(first)
    def _():
        pltpu.make_async_copy(one, to, sem).start()

    @pl.when(jnp.logical_not(first))
    def _():
        pltpu.make_async_copy(two, to, sem).start()


def rows_of(bin_):
    return pl.ds(bin_ * 2, 2)


def crossing(pairs, zl):
    flags = []
    alone, doubles = jnp.int32(0), jnp.int32(0)
    for p in range(NPAIR):
        a, b = (pairs[2 * p + side] // (CORE * OWN_BLKS) == zl for side in range(2))
        one, both = jnp.where(a != b, 1, 0), jnp.where(a & b, 1, 0)
        flags.append((one, both))
        alone, doubles = alone + one, doubles + 2 * both
    moved = jnp.maximum(doubles - alone, 0) // 2
    inner, outer, seen = jnp.int32(0), jnp.int32(0), jnp.int32(0)
    plan = []
    for one, both in flags:
        at = inner
        inner = inner + one
        bins = []
        for _ in range(BINS):
            near = seen < moved
            bins.append((near, jnp.where(near, inner, outer)))
            inner = inner + jnp.where(near, both, 0)
            outer = outer + jnp.where(near, 0, both)
            seen = seen + both
        plan.append((one == 1, at, both == 1, bins))
    return inner, outer, plan


def couples_kernel(pairs_ref, out_ref):
    most = jnp.int32(LEAST)
    for zl in range(ZL):
        inner, outer, _ = crossing(pairs_ref, zl)
        most = jnp.maximum(most, jnp.maximum(inner, outer))
    out_ref[0] = most


def couples_of(pairs):
    return pl.pallas_call(
        couples_kernel,
        in_specs=[smem()],
        out_specs=smem(),
        out_shape=jax.ShapeDtypeStruct((1,), jnp.int32),
        name="couples",
    )(pairs)[0]


def sending_kernel(place_ref, pairs_ref, mine_ref, other_ref, inner_ref, outer_ref, sems):
    zl, core = place_ref[0], place_ref[1]
    plan = crossing(pairs_ref, zl)[2]
    for start in (True, False):
        for p in range(NPAIR):
            blocks = (pairs_ref[2 * p], pairs_ref[2 * p + 1])
            one, at, both, bins = plan[p]
            here_a = whose(blocks[0], zl, core)[0]
            lone = jnp.where(here_a, blocks[0], blocks[1])

            def move(block, bin_, to, sem, start=start):
                own = whose(block, zl, core)[1]
                source = (block % OWN_BLKS, slice(None), rows_of(bin_))
                if start:
                    copy_either(own, mine_ref.at[source], other_ref.at[source], to, sem)
                else:
                    pltpu.make_async_copy(mine_ref.at[source], to, sem).wait()

            for bin_ in range(BINS):
                near, slot = bins[bin_]
                number = (p * BINS + bin_) * 2

                @pl.when(one)
                def _(lone=lone, bin_=bin_, at=at, number=number, move=move):
                    move(lone, bin_, inner_ref.at[at, bin_], sems.at[number])

                for side in range(2):

                    @pl.when(both & near)
                    def _(block=blocks[side], bin_=bin_, slot=slot, side=side, number=number, move=move):
                        move(block, bin_, inner_ref.at[slot, side], sems.at[number + side])

                    @pl.when(both & jnp.logical_not(near))
                    def _(block=blocks[side], bin_=bin_, slot=slot, side=side, number=number, move=move):
                        move(block, bin_, outer_ref.at[slot, side], sems.at[number + side])


def sending(couples, place, pairs, mine, other):
    out = jax.ShapeDtypeStruct((couples, 2, YX, 2, OWN_SEGS, BLK), BF16)
    return pl.pallas_call(
        sending_kernel,
        in_specs=[smem(), smem(), hbm(), hbm()],
        out_specs=[hbm(), hbm()],
        out_shape=[out, out],
        scratch_shapes=[pltpu.SemaphoreType.DMA((NPAIR * BINS * 2,))],
        compiler_params=pltpu.CompilerParams(vmem_limit_bytes=4 * MIB),
        cost_estimate=pl.CostEstimate(flops=0, bytes_accessed=4 * MIB, transcendentals=0),
        name="sending",
    )(place, pairs, mine, other)


def places(pairs_ref, zl, core):
    for p in range(NPAIR):
        for side in range(2):
            block = pairs_ref[2 * p + side]
            for bin_ in range(BINS):
                yield (2 * p + side) * BINS + bin_, p, side, bin_, block, whose(block, zl, core)[0]


def kept_kernel(place_ref, pairs_ref, chip_ref, out_ref, sems):
    zl, core = place_ref[0], place_ref[1]
    for start in (True, False):
        for number, p, side, bin_, block, here in places(pairs_ref, zl, core):
            at = (block % (CORE * OWN_BLKS), slice(None), rows_of(bin_))
            copy = pltpu.make_async_copy(chip_ref.at[at], out_ref.at[:, p, side, rows_of(bin_)], sems.at[number])

            @pl.when(here)
            def _(start=start, copy=copy):
                if start:
                    copy.start()
                else:
                    copy.wait()


def came_kernel(place_ref, pairs_ref, inner_ref, outer_ref, kept_ref, out_ref, sems):
    zl, core = place_ref[0], place_ref[1]
    plan = crossing(pairs_ref, 1 - zl)[2]
    for start in (True, False):
        for number, p, side, bin_, _, here in places(pairs_ref, zl, core):
            one, at, both, bins = plan[p]
            near, slot = bins[bin_]
            to = out_ref.at[:, p, side, rows_of(bin_)]

            def move(source, to=to, sem=sems.at[number], start=start):
                copy = pltpu.make_async_copy(source, to, sem)
                if start:
                    copy.start()
                else:
                    copy.wait()

            @pl.when(one & jnp.logical_not(here))
            def _(move=move, at=at, bin_=bin_):
                move(inner_ref.at[at, bin_])

            @pl.when(both & near)
            def _(move=move, slot=slot, side=side):
                move(inner_ref.at[slot, side])

            @pl.when(both & jnp.logical_not(near))
            def _(move=move, slot=slot, side=side):
                move(outer_ref.at[slot, side])


def sides_of(kernel, name, place, pairs, *arrays):
    return pl.pallas_call(
        kernel,
        in_specs=[smem(), smem()] + [hbm()] * len(arrays),
        out_specs=hbm(),
        out_shape=jax.ShapeDtypeStruct((YX, NPAIR, 2, 2 * BINS, OWN_SEGS, BLK), BF16),
        scratch_shapes=[pltpu.SemaphoreType.DMA((2 * NPAIR * BINS,))],
        input_output_aliases={4: 0} if len(arrays) == 3 else {},
        compiler_params=pltpu.CompilerParams(vmem_limit_bytes=4 * MIB),
        cost_estimate=pl.CostEstimate(flops=0, bytes_accessed=3 * MIB, transcendentals=0),
        name=name,
    )(place, pairs, *arrays)


def products_kernel(factors_ref, out_ref, part_ref, rows_ref):
    length = YX * OWN_SEGS
    for p in range(NPAIR):
        for bin_ in range(BINS):
            x, y = (
                jnp.concatenate(
                    [factors_ref[:, p, side, 2 * bin_ + c].reshape(length, BLK) for c in range(2)], axis=1
                )
                for side in range(2)
            )
            g = lax.dot_general(x, y, (((0,), (0,)), ((), ())), preferred_element_type=F32)
            part_ref[0] = g[:BLK, :BLK] + g[BLK:, BLK:]
            part_ref[1] = g[BLK:, :BLK] - g[:BLK, BLK:]
            for c in range(2):
                for r in range(2):
                    at = p * 8 + r * 4 + bin_ * 2 + c
                    rows_ref[pl.ds(at, BLK // 2, stride=8 * NPAIR), :] = part_ref[c, pl.ds(r, BLK // 2, stride=2), :]
    out_ref[...] = rows_ref[...].astype(BF16)


def products(gathered):
    return pl.pallas_call(
        products_kernel,
        in_specs=[vmem()],
        out_specs=vmem(),
        out_shape=jax.ShapeDtypeStruct((BLK // 2 * NPAIR * 8, BLK), BF16),
        scratch_shapes=[pltpu.VMEM((2, BLK, BLK), F32), pltpu.VMEM((BLK // 2 * NPAIR * 8, BLK), F32)],
        compiler_params=pltpu.CompilerParams(vmem_limit_bytes=16 * MIB),
        cost_estimate=pl.CostEstimate(flops=2 * 8 * 256**3, bytes_accessed=3 * MIB, transcendentals=0),
        name="products",
    )(gathered)


def lags_kernel(scale, shares_ref, back_ref, out_ref):
    total = shares_ref[0].astype(F32)
    for z in range(1, ZH):
        total += shares_ref[z].astype(F32)
    stacked = total.astype(BF16)
    for r in range(2):
        lagged = lax.dot_general(stacked, back_ref[r], (((0,), (0,)), ((), ())), preferred_element_type=F32)
        out_ref[0, r * BLK : (r + 1) * BLK, :] = lagged * scale


def lags(shares, total):
    rows = inverse_rows()
    back = np.zeros((2, rows.shape[0], 2, 2 * BINS, NFFT), np.float32)
    for r in range(2):
        back[r, :, r] = rows
    back = jnp.asarray(back.reshape(2, 4 * NBAND, NFFT), BF16)
    scale = 1.0 / math.sqrt(total * NBAND)
    return pl.pallas_call(
        lambda *refs: lags_kernel(scale, *refs),
        in_specs=[vmem(), vmem()],
        out_specs=vmem(),
        out_shape=jax.ShapeDtypeStruct((1, 2 * BLK, NFFT), F32),
        compiler_params=pltpu.CompilerParams(vmem_limit_bytes=16 * MIB),
        cost_estimate=pl.CostEstimate(flops=4 * 512 * 128 * 512, bytes_accessed=2 * MIB, transcendentals=0),
        name="lags",
    )(shares, back)


def swap(x, axis):
    return lax.ppermute(x, axis, [(0, 1), (1, 0)])


def swap_outer(x):
    turns = []
    for zh in range(ZH):
        turns.append((zh * ZL, (zh - 1) % ZH * ZL + 1))
        turns.append((zh * ZL + 1, (zh + 1) % ZH * ZL))
    return lax.ppermute(x, ("zh", "zl"), turns)


def both_sides(couples, place, pairs, chan, keep, records, tables, mine_far, other_far):
    inner, outer = sending(couples, place, pairs, mine_far, other_far)
    later, *_ = lax.optimization_barrier((chan, inner))
    inner, outer = swap(inner, "zl"), swap_outer(outer)
    (chip,) = spectra(0, (CORE,), 1, "spectra_near", later, keep, records, tables)
    chip = lax.all_to_all(chip, "core", 0, 0, tiled=True)
    chip = chip.reshape((CORE * OWN_BLKS,) + chip.shape[2:])
    kept = sides_of(kept_kernel, "kept", place, pairs, chip)
    return sides_of(came_kernel, "came", place, pairs, inner, outer, kept)


def shards(records, keep, pairs):
    zl, core = lax.axis_index("zl"), lax.axis_index("core")
    place = jnp.stack([zl, core]).astype(jnp.int32)
    chan = (zl * CORE + core).astype(jnp.int32).reshape(1)
    flat = pairs.reshape(-1)
    tables = jnp.asarray(forward_tables(), BF16)
    mine_far, theirs_far = spectra(1, (), 2, "spectra_far", chan, keep, records, tables)
    other_far = swap(theirs_far, "core")
    sides = lax.switch(
        couples_of(flat) - LEAST,
        [functools.partial(both_sides, couples) for couples in range(LEAST, NPAIR + 1)],
        *(place, flat, chan, keep, records, tables, mine_far, other_far),
    )
    gathered = lax.all_to_all(sides, ("y", "x"), 0, 0, tiled=True)
    shares = products(gathered).reshape(ZH * YX * NPAIR, 8, BLK)
    shares = lax.all_to_all(shares, ("zh", "y", "x", "zl", "core"), 0, 0, tiled=True)
    total = records.shape[0] * ZH * YX
    return lags(shares.reshape(ZH, YX * NPAIR * 8, BLK), total)


def solution(mesh):
    fine = Mesh(mesh.devices.reshape(ZH, 4, 4, ZL, CORE), ("zh", "y", "x", "zl", "core"))
    win, chan = ("zh", "y", "x"), ("zl", "core")
    in_specs = (P(win, chan, None), P(win), P())
    out_specs = P(chan, win, None)
    return jax.shard_map(shards, mesh=fine, in_specs=in_specs, out_specs=out_specs, check_vma=False)
```

```python
import functools
import math

import jax
import jax.numpy as jnp
import numpy as np
from jax import lax
from jax.experimental import pallas as pl
from jax.experimental.pallas import tpu as pltpu
from jax.sharding import Mesh
from jax.sharding import PartitionSpec as P

BLK = 128
NBAND = 128
SEG = 256
NFFT = 512
NPAIR = 4
ZH, YX, ZL, CORE = 4, 16, 2, 2
OWN_SEGS = 16
OWN_BLKS = 4
BINS = 2
LEAST = 2
F32, BF16 = jnp.float32, jnp.bfloat16
MIB = 1 << 20


def bins_of(half, quarter):
    first = (half * ZL + quarter) * YX * BINS
    return (1 + first + np.arange(YX * BINS)).reshape(YX, BINS)


def forward_rows(bins):
    phase = (bins.reshape(-1, 1) * np.arange(SEG)[None, :]) % NFFT
    angle = phase.astype(np.float64) * (2.0 * math.pi / NFFT)
    both = np.stack([np.cos(angle), -np.sin(angle)], axis=1)
    return (both.reshape(-1, SEG) / math.sqrt(SEG)).astype(np.float32)


def forward_tables():
    tables = []
    for zl in range(ZL):
        for core in range(CORE):
            near = [bins_of(0, zl), bins_of(1, zl)]
            far = [bins_of(core, zl ^ 1), bins_of(core ^ 1, zl ^ 1)]
            tables.append(np.concatenate([forward_rows(bins) for bins in near + far]))
    return np.stack(tables)


def inverse_rows():
    order = np.stack(
        [np.stack([bins_of(core, zl) for core in range(CORE)], axis=1) for zl in range(ZL)], axis=1
    )
    phase = (order.reshape(-1, 1) * (np.arange(NFFT)[None, :] - NFFT // 2)) % NFFT
    angle = phase.astype(np.float64) * (2.0 * math.pi / NFFT)
    both = np.stack([np.cos(angle), -np.sin(angle)], axis=1)
    return both.reshape(-1, 2 * BINS, NFFT).astype(np.float32)


def named(step, chan_ref, pairs_ref):
    marks = []
    for k in range(OWN_BLKS):
        block = chan_ref[0] * OWN_BLKS + k
        mark = jnp.int32(0)
        for p in range(NPAIR):
            for side in range(2):
                mark = jnp.where(pairs_ref[side, p] == block, 1, mark)
        marks.append(mark)
    count = sum(marks[1:], marks[0])
    want = jnp.minimum(step, jnp.maximum(count - 1, 0))
    at, seen = jnp.int32(0), jnp.int32(0)
    for k, mark in enumerate(marks):
        at = jnp.where((mark == 1) & (seen == want), k, at)
        seen = seen + mark
    return at, step < count


def spectra_kernel(chan_ref, keep_ref, pairs_ref, *refs):
    there = named(pl.program_id(0), chan_ref, pairs_ref)[1]

    @pl.when(there)
    def _():
        block_spectra(keep_ref, *refs)


def block_spectra(keep_ref, records_ref, table_ref, taper_ref, *refs):
    outs, rows_ref = refs[:-1], refs[-1]
    table = table_ref[0]
    taper = taper_ref[...]
    for s in range(OWN_SEGS):
        samples = records_ref[s]
        centred = samples - jnp.mean(samples, axis=1, keepdims=True)
        power = jnp.mean(centred * centred, axis=1, keepdims=True)
        weight = keep_ref[s].astype(F32)
        prepared = (centred * (lax.rsqrt(power + 1e-06) * weight) * taper).astype(BF16)
        spectra = lax.dot_general(table, prepared, (((1,), (1,)), ((), ())), preferred_element_type=F32)
        rows_ref[pl.ds(s, NBAND, stride=OWN_SEGS), :] = spectra
    length = NBAND * OWN_SEGS // len(outs)
    for n, out_ref in enumerate(outs):
        part = rows_ref[n * length : (n + 1) * length, :]
        out_ref[...] = part.astype(BF16).reshape(out_ref.shape)


def in_hbm(x):
    return pltpu.with_memory_space_constraint(x, pltpu.HBM)


def spectra(half, lead, count, name, chan, keep, pairs, records, tables):
    steps = np.arange(SEG, dtype=np.float64)
    taper = jnp.asarray((0.5 - 0.5 * np.cos(2.0 * math.pi * (steps + 0.5) / SEG)).astype(np.float32)[None])
    tail = (YX, 2 * BINS, OWN_SEGS, BLK)
    out = jax.ShapeDtypeStruct(lead + (OWN_BLKS,) + tail, BF16)
    out_spec = pl.BlockSpec(
        lead + (1,) + tail, lambda b, c, k, q: (0,) * len(lead) + (named(b, c, q)[0], 0, 0, 0, 0)
    )
    return pl.pallas_call(
        spectra_kernel,
        grid_spec=pltpu.PrefetchScalarGridSpec(
            num_scalar_prefetch=3,
            grid=(OWN_BLKS,),
            in_specs=[
                pl.BlockSpec((OWN_SEGS, BLK, SEG), lambda b, c, k, q: (0, named(b, c, q)[0], 0)),
                pl.BlockSpec((1, NBAND, SEG), lambda b, c, k, q: (c[0], half, 0)),
                pl.BlockSpec((1, SEG), lambda b, *_: (0, 0)),
            ],
            out_specs=[out_spec] * count,
            scratch_shapes=[pltpu.VMEM((NBAND * OWN_SEGS, BLK), F32)],
        ),
        out_shape=[out] * count,
        compiler_params=pltpu.CompilerParams(vmem_limit_bytes=16 * MIB),
        cost_estimate=pl.CostEstimate(flops=8192 * 256 * 256, bytes_accessed=11 * MIB, transcendentals=8192),
        name=name,
    )(chan, keep, pairs, in_hbm(records), in_hbm(tables), in_hbm(taper))


def whose(block, zl, core):
    return block // (CORE * OWN_BLKS) == zl, (block // OWN_BLKS) % CORE == core


def vmem():
    return pl.BlockSpec(memory_space=pltpu.VMEM)


def smem():
    return pl.BlockSpec(memory_space=pltpu.SMEM)


def hbm():
    return pl.BlockSpec(memory_space=pltpu.HBM)


def copy_either(first, one, two, to, sem):
    @pl.when(first)
    def _():
        pltpu.make_async_copy(one, to, sem).start()

    @pl.when(jnp.logical_not(first))
    def _():
        pltpu.make_async_copy(two, to, sem).start()


def rows_of(bin_):
    return pl.ds(bin_ * 2, 2)


def crossing(pairs, zl):
    flags = []
    alone, doubles = jnp.int32(0), jnp.int32(0)
    for p in range(NPAIR):
        a, b = (pairs[side, p] // (CORE * OWN_BLKS) == zl for side in range(2))
        one, both = jnp.where(a != b, 1, 0), jnp.where(a & b, 1, 0)
        flags.append((one, both))
        alone, doubles = alone + one, doubles + 2 * both
    moved = jnp.maximum(doubles - alone, 0) // 2
    inner, outer, seen = jnp.int32(0), jnp.int32(0), jnp.int32(0)
    plan = []
    for one, both in flags:
        at = inner
        inner = inner + one
        bins = []
        for _ in range(BINS):
            near = seen < moved
            bins.append((near, jnp.where(near, inner, outer)))
            inner = inner + jnp.where(near, both, 0)
            outer = outer + jnp.where(near, 0, both)
            seen = seen + both
        plan.append((one == 1, at, both == 1, bins))
    return inner, outer, plan


def couples_kernel(pairs_ref, out_ref):
    most = jnp.int32(LEAST)
    for zl in range(ZL):
        inner, outer, _ = crossing(pairs_ref, zl)
        most = jnp.maximum(most, jnp.maximum(inner, outer))
    out_ref[0] = most


def couples_of(pairs):
    return pl.pallas_call(
        couples_kernel,
        in_specs=[smem()],
        out_specs=smem(),
        out_shape=jax.ShapeDtypeStruct((1,), jnp.int32),
        name="couples",
    )(pairs)[0]


def sending_kernel(place_ref, pairs_ref, mine_ref, other_ref, inner_ref, outer_ref, sems):
    zl, core = place_ref[0], place_ref[1]
    plan = crossing(pairs_ref, zl)[2]
    for start in (True, False):
        for p in range(NPAIR):
            blocks = (pairs_ref[0, p], pairs_ref[1, p])
            one, at, both, bins = plan[p]
            here_a = whose(blocks[0], zl, core)[0]
            lone = jnp.where(here_a, blocks[0], blocks[1])

            def move(block, bin_, to, sem, start=start):
                own = whose(block, zl, core)[1]
                source = (block % OWN_BLKS, slice(None), rows_of(bin_))
                if start:
                    copy_either(own, mine_ref.at[source], other_ref.at[source], to, sem)
                else:
                    pltpu.make_async_copy(mine_ref.at[source], to, sem).wait()

            for bin_ in range(BINS):
                near, slot = bins[bin_]
                number = (p * BINS + bin_) * 2

                @pl.when(one)
                def _(lone=lone, bin_=bin_, at=at, number=number, move=move):
                    move(lone, bin_, inner_ref.at[at, bin_], sems.at[number])

                for side in range(2):

                    @pl.when(both & near)
                    def _(block=blocks[side], bin_=bin_, slot=slot, side=side, number=number, move=move):
                        move(block, bin_, inner_ref.at[slot, side], sems.at[number + side])

                    @pl.when(both & jnp.logical_not(near))
                    def _(block=blocks[side], bin_=bin_, slot=slot, side=side, number=number, move=move):
                        move(block, bin_, outer_ref.at[slot, side], sems.at[number + side])


def sending(couples, place, pairs, mine, other):
    out = jax.ShapeDtypeStruct((couples, 2, YX, 2, OWN_SEGS, BLK), BF16)
    return pl.pallas_call(
        sending_kernel,
        in_specs=[smem(), smem(), hbm(), hbm()],
        out_specs=[hbm(), hbm()],
        out_shape=[out, out],
        scratch_shapes=[pltpu.SemaphoreType.DMA((NPAIR * BINS * 2,))],
        compiler_params=pltpu.CompilerParams(vmem_limit_bytes=4 * MIB),
        cost_estimate=pl.CostEstimate(flops=0, bytes_accessed=4 * MIB, transcendentals=0),
        name="sending",
    )(place, pairs, mine, other)


def places(pairs_ref, zl, core):
    for p in range(NPAIR):
        for side in range(2):
            block = pairs_ref[side, p]
            for bin_ in range(BINS):
                yield (2 * p + side) * BINS + bin_, p, side, bin_, block, whose(block, zl, core)[0]


def kept_kernel(place_ref, pairs_ref, chip_ref, out_ref, sems):
    zl, core = place_ref[0], place_ref[1]
    for start in (True, False):
        for number, p, side, bin_, block, here in places(pairs_ref, zl, core):
            at = (block % (CORE * OWN_BLKS), slice(None), rows_of(bin_))
            copy = pltpu.make_async_copy(chip_ref.at[at], out_ref.at[:, p, side, rows_of(bin_)], sems.at[number])

            @pl.when(here)
            def _(start=start, copy=copy):
                if start:
                    copy.start()
                else:
                    copy.wait()


def came_kernel(place_ref, pairs_ref, inner_ref, outer_ref, kept_ref, out_ref, sems):
    zl, core = place_ref[0], place_ref[1]
    plan = crossing(pairs_ref, 1 - zl)[2]
    for start in (True, False):
        for number, p, side, bin_, _, here in places(pairs_ref, zl, core):
            one, at, both, bins = plan[p]
            near, slot = bins[bin_]
            to = out_ref.at[:, p, side, rows_of(bin_)]

            def move(source, to=to, sem=sems.at[number], start=start):
                copy = pltpu.make_async_copy(source, to, sem)
                if start:
                    copy.start()
                else:
                    copy.wait()

            @pl.when(one & jnp.logical_not(here))
            def _(move=move, at=at, bin_=bin_):
                move(inner_ref.at[at, bin_])

            @pl.when(both & near)
            def _(move=move, slot=slot, side=side):
                move(inner_ref.at[slot, side])

            @pl.when(both & jnp.logical_not(near))
            def _(move=move, slot=slot, side=side):
                move(outer_ref.at[slot, side])


def sides_of(kernel, name, place, pairs, *arrays):
    return pl.pallas_call(
        kernel,
        in_specs=[smem(), smem()] + [hbm()] * len(arrays),
        out_specs=hbm(),
        out_shape=jax.ShapeDtypeStruct((YX, NPAIR, 2, 2 * BINS, OWN_SEGS, BLK), BF16),
        scratch_shapes=[pltpu.SemaphoreType.DMA((2 * NPAIR * BINS,))],
        input_output_aliases={4: 0} if len(arrays) == 3 else {},
        compiler_params=pltpu.CompilerParams(vmem_limit_bytes=4 * MIB),
        cost_estimate=pl.CostEstimate(flops=0, bytes_accessed=3 * MIB, transcendentals=0),
        name=name,
    )(place, pairs, *arrays)


def products_kernel(factors_ref, out_ref, part_ref, rows_ref):
    length = YX * OWN_SEGS
    for p in range(NPAIR):
        for bin_ in range(BINS):
            x, y = (
                jnp.concatenate(
                    [factors_ref[:, p, side, 2 * bin_ + c].reshape(length, BLK) for c in range(2)], axis=1
                )
                for side in range(2)
            )
            g = lax.dot_general(x, y, (((0,), (0,)), ((), ())), preferred_element_type=F32)
            part_ref[0] = g[:BLK, :BLK] + g[BLK:, BLK:]
            part_ref[1] = g[BLK:, :BLK] - g[:BLK, BLK:]
            for c in range(2):
                for r in range(2):
                    at = p * 8 + r * 4 + bin_ * 2 + c
                    rows_ref[pl.ds(at, BLK // 2, stride=8 * NPAIR), :] = part_ref[c, pl.ds(r, BLK // 2, stride=2), :]
    out_ref[...] = rows_ref[...].astype(BF16)


def products(gathered):
    return pl.pallas_call(
        products_kernel,
        in_specs=[vmem()],
        out_specs=vmem(),
        out_shape=jax.ShapeDtypeStruct((BLK // 2 * NPAIR * 8, BLK), BF16),
        scratch_shapes=[pltpu.VMEM((2, BLK, BLK), F32), pltpu.VMEM((BLK // 2 * NPAIR * 8, BLK), F32)],
        compiler_params=pltpu.CompilerParams(vmem_limit_bytes=16 * MIB),
        cost_estimate=pl.CostEstimate(flops=2 * 8 * 256**3, bytes_accessed=3 * MIB, transcendentals=0),
        name="products",
    )(gathered)


def lags_kernel(scale, shares_ref, back_ref, out_ref):
    total = shares_ref[0].astype(F32)
    for z in range(1, ZH):
        total += shares_ref[z].astype(F32)
    stacked = total.astype(BF16)
    for r in range(2):
        lagged = lax.dot_general(stacked, back_ref[r], (((0,), (0,)), ((), ())), preferred_element_type=F32)
        out_ref[0, r * BLK : (r + 1) * BLK, :] = lagged * scale


def lags(shares, total):
    rows = inverse_rows()
    back = np.zeros((2, rows.shape[0], 2, 2 * BINS, NFFT), np.float32)
    for r in range(2):
        back[r, :, r] = rows
    back = jnp.asarray(back.reshape(2, 4 * NBAND, NFFT), BF16)
    scale = 1.0 / math.sqrt(total * NBAND)
    return pl.pallas_call(
        lambda *refs: lags_kernel(scale, *refs),
        in_specs=[vmem(), vmem()],
        out_specs=vmem(),
        out_shape=jax.ShapeDtypeStruct((1, 2 * BLK, NFFT), F32),
        compiler_params=pltpu.CompilerParams(vmem_limit_bytes=16 * MIB),
        cost_estimate=pl.CostEstimate(flops=4 * 512 * 128 * 512, bytes_accessed=2 * MIB, transcendentals=0),
        name="lags",
    )(shares, back)


def swap(x, axis):
    return lax.ppermute(x, axis, [(0, 1), (1, 0)])


def swap_outer(x):
    turns = []
    for zh in range(ZH):
        turns.append((zh * ZL, (zh - 1) % ZH * ZL + 1))
        turns.append((zh * ZL + 1, (zh + 1) % ZH * ZL))
    return lax.ppermute(x, ("zh", "zl"), turns)


def both_sides(couples, place, pairs, chan, keep, records, tables, mine_far, other_far):
    inner, outer = sending(couples, place, pairs, mine_far, other_far)
    later, *_ = lax.optimization_barrier((chan, inner))
    inner, outer = swap(inner, "zl"), swap_outer(outer)
    (chip,) = spectra(0, (CORE,), 1, "spectra_near", later, keep, pairs, records, tables)
    chip = lax.all_to_all(chip, "core", 0, 0, tiled=True)
    chip = chip.reshape((CORE * OWN_BLKS,) + chip.shape[2:])
    kept = sides_of(kept_kernel, "kept", place, pairs, chip)
    return sides_of(came_kernel, "came", place, pairs, inner, outer, kept)


def shards(records, keep, pairs):
    zl, core = lax.axis_index("zl"), lax.axis_index("core")
    place = jnp.stack([zl, core]).astype(jnp.int32)
    chan = (zl * CORE + core).astype(jnp.int32).reshape(1)
    sides_first = pairs.T
    tables = jnp.asarray(forward_tables(), BF16)
    mine_far, theirs_far = spectra(1, (), 2, "spectra_far", chan, keep, sides_first, records, tables)
    other_far = swap(theirs_far, "core")
    sides = lax.switch(
        couples_of(sides_first) - LEAST,
        [functools.partial(both_sides, couples) for couples in range(LEAST, NPAIR + 1)],
        *(place, sides_first, chan, keep, records, tables, mine_far, other_far),
    )
    gathered = lax.all_to_all(sides, ("y", "x"), 0, 0, tiled=True)
    shares = products(gathered).reshape(ZH * YX * NPAIR, 8, BLK)
    shares = lax.all_to_all(shares, ("zh", "y", "x", "zl", "core"), 0, 0, tiled=True)
    total = records.shape[0] * ZH * YX
    return lags(shares.reshape(ZH, YX * NPAIR * 8, BLK), total)


def solution(mesh):
    fine = Mesh(mesh.devices.reshape(ZH, 4, 4, ZL, CORE), ("zh", "y", "x", "zl", "core"))
    win, chan = ("zh", "y", "x"), ("zl", "core")
    in_specs = (P(win, chan, None), P(win), P())
    out_specs = P(chan, win, None)
    return jax.shard_map(shards, mesh=fine, in_specs=in_specs, out_specs=out_specs, check_vma=False)
```

```python
import functools
import math

import jax
import jax.numpy as jnp
import numpy as np
from jax import lax
from jax.experimental import pallas as pl
from jax.experimental.pallas import tpu as pltpu
from jax.sharding import Mesh
from jax.sharding import PartitionSpec as P

BLK = 128
NBAND = 128
SEG = 256
NFFT = 512
NPAIR = 4
ZH, YX, ZL, CORE = 4, 16, 2, 2
OWN_SEGS = 16
OWN_BLKS = 4
BINS = 2
LEAST = 2
F32, BF16 = jnp.float32, jnp.bfloat16
MIB = 1 << 20


def bins_of(half, quarter):
    first = (half * ZL + quarter) * YX * BINS
    return (1 + first + np.arange(YX * BINS)).reshape(YX, BINS)


def forward_rows(bins):
    phase = (bins.reshape(-1, 1) * np.arange(SEG)[None, :]) % NFFT
    angle = phase.astype(np.float64) * (2.0 * math.pi / NFFT)
    both = np.stack([np.cos(angle), -np.sin(angle)], axis=1)
    return (both.reshape(-1, SEG) / math.sqrt(SEG)).astype(np.float32)


def forward_tables():
    tables = []
    for zl in range(ZL):
        for core in range(CORE):
            near = [bins_of(0, zl), bins_of(1, zl)]
            far = [bins_of(core, zl ^ 1), bins_of(core ^ 1, zl ^ 1)]
            tables.append(np.concatenate([forward_rows(bins) for bins in near + far]))
    return np.stack(tables)


def inverse_rows():
    order = np.stack(
        [np.stack([bins_of(core, zl) for core in range(CORE)], axis=1) for zl in range(ZL)], axis=1
    )
    phase = (order.reshape(-1, 1) * (np.arange(NFFT)[None, :] - NFFT // 2)) % NFFT
    angle = phase.astype(np.float64) * (2.0 * math.pi / NFFT)
    both = np.stack([np.cos(angle), -np.sin(angle)], axis=1)
    return both.reshape(-1, 2 * BINS, NFFT).astype(np.float32)


def named(step, chan_ref, pairs_ref):
    marks = []
    for k in range(OWN_BLKS):
        block = chan_ref[0] * OWN_BLKS + k
        mark = jnp.int32(0)
        for p in range(NPAIR):
            for side in range(2):
                mark = jnp.where(pairs_ref[side, p] == block, 1, mark)
        marks.append(mark)
    count = sum(marks[1:], marks[0])
    want = jnp.minimum(step, jnp.maximum(count - 1, 0))
    at, seen = jnp.int32(0), jnp.int32(0)
    for k, mark in enumerate(marks):
        at = jnp.where((mark == 1) & (seen == want), k, at)
        seen = seen + mark
    return at, step < count


def spectra_kernel(chan_ref, keep_ref, pairs_ref, *refs):
    there = named(pl.program_id(0), chan_ref, pairs_ref)[1]

    @pl.when(there)
    def _():
        block_spectra(keep_ref, *refs)


def block_spectra(keep_ref, records_ref, table_ref, taper_ref, *refs):
    outs, rows_ref = refs[:-1], refs[-1]
    table = table_ref[0]
    taper = taper_ref[...]
    for s in range(OWN_SEGS):
        samples = records_ref[s]
        centred = samples - jnp.mean(samples, axis=1, keepdims=True)
        power = jnp.mean(centred * centred, axis=1, keepdims=True)
        weight = keep_ref[s].astype(F32)
        prepared = (centred * (lax.rsqrt(power + 1e-06) * weight) * taper).astype(BF16)
        spectra = lax.dot_general(table, prepared, (((1,), (1,)), ((), ())), preferred_element_type=F32)
        rows_ref[pl.ds(s, NBAND, stride=OWN_SEGS), :] = spectra
    length = NBAND * OWN_SEGS // len(outs)
    for n, out_ref in enumerate(outs):
        part = rows_ref[n * length : (n + 1) * length, :]
        out_ref[...] = part.astype(BF16).reshape(out_ref.shape)


def in_hbm(x):
    return pltpu.with_memory_space_constraint(x, pltpu.HBM)


def spectra(half, lead, count, name, chan, keep, pairs, records, tables):
    steps = np.arange(SEG, dtype=np.float64)
    taper = jnp.asarray((0.5 - 0.5 * np.cos(2.0 * math.pi * (steps + 0.5) / SEG)).astype(np.float32)[None])
    tail = (YX, 2 * BINS, OWN_SEGS, BLK)
    out = jax.ShapeDtypeStruct(lead + (OWN_BLKS,) + tail, BF16)
    out_spec = pl.BlockSpec(
        lead + (1,) + tail, lambda b, c, k, q: (0,) * len(lead) + (named(b, c, q)[0], 0, 0, 0, 0)
    )
    return pl.pallas_call(
        spectra_kernel,
        grid_spec=pltpu.PrefetchScalarGridSpec(
            num_scalar_prefetch=3,
            grid=(OWN_BLKS,),
            in_specs=[
                pl.BlockSpec((OWN_SEGS, BLK, SEG), lambda b, c, k, q: (0, named(b, c, q)[0], 0)),
                pl.BlockSpec((1, NBAND, SEG), lambda b, c, k, q: (c[0], half, 0)),
                pl.BlockSpec((1, SEG), lambda b, *_: (0, 0)),
            ],
            out_specs=[out_spec] * count,
            scratch_shapes=[pltpu.VMEM((NBAND * OWN_SEGS, BLK), F32)],
        ),
        out_shape=[out] * count,
        compiler_params=pltpu.CompilerParams(vmem_limit_bytes=16 * MIB),
        cost_estimate=pl.CostEstimate(flops=8192 * 256 * 256, bytes_accessed=11 * MIB, transcendentals=8192),
        name=name,
    )(chan, keep, pairs, in_hbm(records), in_hbm(tables), in_hbm(taper))


def whose(block, zl, core):
    return block // (CORE * OWN_BLKS) == zl, (block // OWN_BLKS) % CORE == core


def vmem():
    return pl.BlockSpec(memory_space=pltpu.VMEM)


def smem():
    return pl.BlockSpec(memory_space=pltpu.SMEM)


def hbm():
    return pl.BlockSpec(memory_space=pltpu.HBM)


def copy_either(first, one, two, to, sem):
    @pl.when(first)
    def _():
        pltpu.make_async_copy(one, to, sem).start()

    @pl.when(jnp.logical_not(first))
    def _():
        pltpu.make_async_copy(two, to, sem).start()


def rows_of(bin_):
    return pl.ds(bin_ * 2, 2)


def crossing(pairs, zl):
    flags = []
    alone, doubles = jnp.int32(0), jnp.int32(0)
    for p in range(NPAIR):
        a, b = (pairs[side, p] // (CORE * OWN_BLKS) == zl for side in range(2))
        one, both = jnp.where(a != b, 1, 0), jnp.where(a & b, 1, 0)
        flags.append((one, both))
        alone, doubles = alone + one, doubles + 2 * both
    moved = jnp.maximum(doubles - alone, 0) // 2
    inner, outer, seen = jnp.int32(0), jnp.int32(0), jnp.int32(0)
    plan = []
    for one, both in flags:
        at = inner
        inner = inner + one
        bins = []
        for _ in range(BINS):
            near = seen < moved
            bins.append((near, jnp.where(near, inner, outer)))
            inner = inner + jnp.where(near, both, 0)
            outer = outer + jnp.where(near, 0, both)
            seen = seen + both
        plan.append((one == 1, at, both == 1, bins))
    return inner, outer, plan


def couples_kernel(pairs_ref, out_ref):
    most = jnp.int32(LEAST)
    for zl in range(ZL):
        inner, outer, _ = crossing(pairs_ref, zl)
        most = jnp.maximum(most, jnp.maximum(inner, outer))
    out_ref[0] = most


def couples_of(pairs):
    return pl.pallas_call(
        couples_kernel,
        in_specs=[smem()],
        out_specs=smem(),
        out_shape=jax.ShapeDtypeStruct((1,), jnp.int32),
        name="couples",
    )(pairs)[0]


def sending_kernel(place_ref, pairs_ref, mine_ref, other_ref, inner_ref, outer_ref, sems):
    zl, core = place_ref[0], place_ref[1]
    plan = crossing(pairs_ref, zl)[2]

    def source(ref, block, bin_):
        return ref.at[block % OWN_BLKS, :, rows_of(bin_)]

    def move(block, bin_, to, sem):
        own = whose(block, zl, core)[1]
        copy_either(own, source(mine_ref, block, bin_), source(other_ref, block, bin_), to, sem)

    def await_all(p):
        for n in range(2 * BINS):
            pltpu.make_async_copy(source(mine_ref, 0, 0), inner_ref.at[0, 0], sems.at[p * BINS * 2 + n]).wait()

    for p in range(NPAIR):
        blocks = (pairs_ref[0, p], pairs_ref[1, p])
        one, at, both, bins = plan[p]

        @pl.when(one)
        def _(p=p, blocks=blocks, at=at):
            lone = jnp.where(whose(blocks[0], zl, core)[0], blocks[0], blocks[1])
            for bin_ in range(BINS):
                move(lone, bin_, inner_ref.at[at, bin_], sems.at[p * BINS * 2 + bin_])

        @pl.when(both)
        def _(p=p, blocks=blocks, bins=bins):
            for bin_ in range(BINS):
                near, slot = bins[bin_]
                for ref, chosen in ((inner_ref, near), (outer_ref, jnp.logical_not(near))):

                    @pl.when(chosen)
                    def _(bin_=bin_, slot=slot, ref=ref):
                        for side in range(2):
                            move(blocks[side], bin_, ref.at[slot, side], sems.at[(p * BINS + bin_) * 2 + side])

    for p in range(NPAIR):
        one, _, both, _ = plan[p]

        @pl.when(one)
        def _(p=p):
            for bin_ in range(BINS):
                sem = sems.at[p * BINS * 2 + bin_]
                pltpu.make_async_copy(source(mine_ref, 0, 0), inner_ref.at[0, 0], sem).wait()

        @pl.when(both)
        def _(p=p):
            await_all(p)


def sending(couples, place, pairs, mine, other):
    out = jax.ShapeDtypeStruct((couples, 2, YX, 2, OWN_SEGS, BLK), BF16)
    return pl.pallas_call(
        sending_kernel,
        in_specs=[smem(), smem(), hbm(), hbm()],
        out_specs=[hbm(), hbm()],
        out_shape=[out, out],
        scratch_shapes=[pltpu.SemaphoreType.DMA((NPAIR * BINS * 2,))],
        compiler_params=pltpu.CompilerParams(vmem_limit_bytes=4 * MIB),
        cost_estimate=pl.CostEstimate(flops=0, bytes_accessed=4 * MIB, transcendentals=0),
        name="sending",
    )(place, pairs, mine, other)


def kept_kernel(place_ref, pairs_ref, chip_ref, out_ref, sems):
    zl, core = place_ref[0], place_ref[1]
    for start in (True, False):
        for p in range(NPAIR):
            for side in range(2):
                block = pairs_ref[side, p]

                @pl.when(whose(block, zl, core)[0])
                def _(start=start, p=p, side=side, block=block):
                    source = chip_ref.at[block % (CORE * OWN_BLKS)]
                    copy = pltpu.make_async_copy(source, out_ref.at[:, p, side], sems.at[2 * p + side])
                    if start:
                        copy.start()
                    else:
                        copy.wait()


def came_kernel(place_ref, pairs_ref, inner_ref, outer_ref, kept_ref, out_ref, sems):
    zl, core = place_ref[0], place_ref[1]
    plan = crossing(pairs_ref, 1 - zl)[2]
    for start in (True, False):
        for p in range(NPAIR):
            one, at, both, bins = plan[p]
            away_a = jnp.logical_not(whose(pairs_ref[0, p], zl, core)[0])

            def go(side, bin_, near, one, two, p=p, start=start):
                to = out_ref.at[:, p, side, rows_of(bin_)]
                sem = sems.at[(2 * p + side) * BINS + bin_]
                if not start:
                    pltpu.make_async_copy(one, to, sem).wait()
                elif two is None:
                    pltpu.make_async_copy(one, to, sem).start()
                else:
                    copy_either(near, one, two, to, sem)

            for side, away in ((0, away_a), (1, jnp.logical_not(away_a))):

                @pl.when(one & away)
                def _(go=go, side=side, at=at):
                    for bin_ in range(BINS):
                        go(side, bin_, None, inner_ref.at[at, bin_], None)

            @pl.when(both)
            def _(go=go, bins=bins, start=start):
                for bin_ in range(BINS):
                    near, slot = bins[bin_]
                    slot = slot if start else 0
                    for side in range(2):
                        go(side, bin_, near, inner_ref.at[slot, side], outer_ref.at[slot, side])


def sides_of(kernel, name, place, pairs, *arrays):
    return pl.pallas_call(
        kernel,
        in_specs=[smem(), smem()] + [hbm()] * len(arrays),
        out_specs=hbm(),
        out_shape=jax.ShapeDtypeStruct((YX, NPAIR, 2, 2 * BINS, OWN_SEGS, BLK), BF16),
        scratch_shapes=[pltpu.SemaphoreType.DMA((2 * NPAIR * BINS,))],
        input_output_aliases={4: 0} if len(arrays) == 3 else {},
        compiler_params=pltpu.CompilerParams(vmem_limit_bytes=4 * MIB),
        cost_estimate=pl.CostEstimate(flops=0, bytes_accessed=3 * MIB, transcendentals=0),
        name=name,
    )(place, pairs, *arrays)


def products_kernel(factors_ref, out_ref, part_ref, rows_ref):
    length = YX * OWN_SEGS
    for p in range(NPAIR):
        for bin_ in range(BINS):
            x, y = (
                jnp.concatenate(
                    [factors_ref[:, p, side, 2 * bin_ + c].reshape(length, BLK) for c in range(2)], axis=1
                )
                for side in range(2)
            )
            g = lax.dot_general(x, y, (((0,), (0,)), ((), ())), preferred_element_type=F32)
            part_ref[0] = g[:BLK, :BLK] + g[BLK:, BLK:]
            part_ref[1] = g[BLK:, :BLK] - g[:BLK, BLK:]
            for c in range(2):
                for r in range(2):
                    at = p * 8 + r * 4 + bin_ * 2 + c
                    rows_ref[pl.ds(at, BLK // 2, stride=8 * NPAIR), :] = part_ref[c, pl.ds(r, BLK // 2, stride=2), :]
    out_ref[...] = rows_ref[...].astype(BF16)


def products(gathered):
    return pl.pallas_call(
        products_kernel,
        in_specs=[vmem()],
        out_specs=vmem(),
        out_shape=jax.ShapeDtypeStruct((BLK // 2 * NPAIR * 8, BLK), BF16),
        scratch_shapes=[pltpu.VMEM((2, BLK, BLK), F32), pltpu.VMEM((BLK // 2 * NPAIR * 8, BLK), F32)],
        compiler_params=pltpu.CompilerParams(vmem_limit_bytes=16 * MIB),
        cost_estimate=pl.CostEstimate(flops=2 * 8 * 256**3, bytes_accessed=3 * MIB, transcendentals=0),
        name="products",
    )(gathered)


def lags_kernel(scale, shares_ref, back_ref, out_ref):
    total = shares_ref[0].astype(F32)
    for z in range(1, ZH):
        total += shares_ref[z].astype(F32)
    stacked = total.astype(BF16)
    for r in range(2):
        lagged = lax.dot_general(stacked, back_ref[r], (((0,), (0,)), ((), ())), preferred_element_type=F32)
        out_ref[0, r * BLK : (r + 1) * BLK, :] = lagged * scale


def backward():
    rows = inverse_rows()
    back = np.zeros((2, rows.shape[0], 2, 2 * BINS, NFFT), np.float32)
    for r in range(2):
        back[r, :, r] = rows
    return jnp.asarray(back.reshape(2, 4 * NBAND, NFFT), BF16)


def lags(shares, back, total):
    scale = 1.0 / math.sqrt(total * NBAND)
    return pl.pallas_call(
        lambda *refs: lags_kernel(scale, *refs),
        in_specs=[vmem(), vmem()],
        out_specs=vmem(),
        out_shape=jax.ShapeDtypeStruct((1, 2 * BLK, NFFT), F32),
        compiler_params=pltpu.CompilerParams(vmem_limit_bytes=16 * MIB),
        cost_estimate=pl.CostEstimate(flops=4 * 512 * 128 * 512, bytes_accessed=2 * MIB, transcendentals=0),
        name="lags",
    )(shares, back)


def swap(x, axis):
    return lax.ppermute(x, axis, [(0, 1), (1, 0)])


def swap_outer(x):
    turns = []
    for zh in range(ZH):
        turns.append((zh * ZL, (zh - 1) % ZH * ZL + 1))
        turns.append((zh * ZL + 1, (zh + 1) % ZH * ZL))
    return lax.ppermute(x, ("zh", "zl"), turns)


def correlations(couples, place, pairs, chan, keep, records, tables, back, mine_far, other_far):
    inner, outer = sending(couples, place, pairs, mine_far, other_far)
    later, *_ = lax.optimization_barrier((chan, inner))
    inner, outer = swap(inner, "zl"), swap_outer(outer)
    (chip,) = spectra(0, (CORE,), 1, "spectra_near", later, keep, pairs, records, tables)
    chip = lax.all_to_all(chip, "core", 0, 0, tiled=True)
    chip = chip.reshape((CORE * OWN_BLKS,) + chip.shape[2:])
    kept = sides_of(kept_kernel, "kept", place, pairs, chip)
    sides = sides_of(came_kernel, "came", place, pairs, inner, outer, kept)
    gathered = lax.all_to_all(sides, ("y", "x"), 0, 0, tiled=True)
    shares = products(gathered).reshape(ZH * YX * NPAIR, 8, BLK)
    shares = lax.all_to_all(shares, ("zh", "y", "x", "zl", "core"), 0, 0, tiled=True)
    return lags(shares.reshape(ZH, YX * NPAIR * 8, BLK), back, records.shape[0] * ZH * YX)


def shards(records, keep, pairs):
    zl, core = lax.axis_index("zl"), lax.axis_index("core")
    place = jnp.stack([zl, core]).astype(jnp.int32)
    chan = (zl * CORE + core).astype(jnp.int32).reshape(1)
    sides_first = pairs.T
    tables = jnp.asarray(forward_tables(), BF16)
    mine_far, theirs_far = spectra(1, (), 2, "spectra_far", chan, keep, sides_first, records, tables)
    other_far = swap(theirs_far, "core")
    return lax.switch(
        couples_of(sides_first) - LEAST,
        [functools.partial(correlations, couples) for couples in range(LEAST, NPAIR + 1)],
        *(place, sides_first, chan, keep, records, tables, backward(), mine_far, other_far),
    )


def solution(mesh):
    fine = Mesh(mesh.devices.reshape(ZH, 4, 4, ZL, CORE), ("zh", "y", "x", "zl", "core"))
    win, chan = ("zh", "y", "x"), ("zl", "core")
    in_specs = (P(win, chan, None), P(win), P())
    out_specs = P(chan, win, None)
    return jax.shard_map(shards, mesh=fine, in_specs=in_specs, out_specs=out_specs, check_vma=False)
```

```python
import functools
import math

import jax
import jax.numpy as jnp
import numpy as np
from jax import lax
from jax.experimental import pallas as pl
from jax.experimental.pallas import tpu as pltpu
from jax.sharding import Mesh
from jax.sharding import PartitionSpec as P

BLK = 128
NBAND = 128
SEG = 256
NFFT = 512
NPAIR = 4
ZH, YX, ZL, CORE = 4, 16, 2, 2
OWN_SEGS = 16
OWN_BLKS = 4
BINS = 2
LEAST = 2
F32, BF16 = jnp.float32, jnp.bfloat16
MIB = 1 << 20


def bins_of(half, quarter):
    first = (half * ZL + quarter) * YX * BINS
    return (1 + first + np.arange(YX * BINS)).reshape(YX, BINS)


def forward_rows(bins):
    phase = (bins.reshape(-1, 1) * np.arange(SEG)[None, :]) % NFFT
    angle = phase.astype(np.float64) * (2.0 * math.pi / NFFT)
    both = np.stack([np.cos(angle), -np.sin(angle)], axis=1)
    return (both.reshape(-1, SEG) / math.sqrt(SEG)).astype(np.float32)


def forward_tables():
    tables = []
    for zl in range(ZL):
        for core in range(CORE):
            near = [bins_of(0, zl), bins_of(1, zl)]
            far = [bins_of(core, zl ^ 1), bins_of(core ^ 1, zl ^ 1)]
            tables.append(np.concatenate([forward_rows(bins) for bins in near + far]))
    return np.stack(tables)


def inverse_rows():
    order = np.stack(
        [np.stack([bins_of(core, zl) for core in range(CORE)], axis=1) for zl in range(ZL)], axis=1
    )
    phase = (order.reshape(-1, 1) * (np.arange(NFFT)[None, :] - NFFT // 2)) % NFFT
    angle = phase.astype(np.float64) * (2.0 * math.pi / NFFT)
    both = np.stack([np.cos(angle), -np.sin(angle)], axis=1)
    return both.reshape(-1, 2 * BINS, NFFT).astype(np.float32)


def named(step, chan_ref, pairs_ref):
    marks = []
    for k in range(OWN_BLKS):
        block = chan_ref[0] * OWN_BLKS + k
        mark = jnp.int32(0)
        for p in range(NPAIR):
            for side in range(2):
                mark = jnp.where(pairs_ref[side, p] == block, 1, mark)
        marks.append(mark)
    count = sum(marks[1:], marks[0])
    want = jnp.minimum(step, jnp.maximum(count - 1, 0))
    at, seen = jnp.int32(0), jnp.int32(0)
    for k, mark in enumerate(marks):
        at = jnp.where((mark == 1) & (seen == want), k, at)
        seen = seen + mark
    return at, step < count


def spectra_kernel(chan_ref, keep_ref, pairs_ref, *refs):
    there = named(pl.program_id(0), chan_ref, pairs_ref)[1]

    @pl.when(there)
    def _():
        block_spectra(keep_ref, *refs)


def block_spectra(keep_ref, records_ref, table_ref, taper_ref, *refs):
    outs, rows_ref = refs[:-1], refs[-1]
    table = table_ref[0]
    taper = taper_ref[...]
    for s in range(OWN_SEGS):
        samples = records_ref[s]
        centred = samples - jnp.mean(samples, axis=1, keepdims=True)
        power = jnp.mean(centred * centred, axis=1, keepdims=True)
        weight = keep_ref[s].astype(F32)
        prepared = (centred * (lax.rsqrt(power + 1e-06) * weight) * taper).astype(BF16)
        spectra = lax.dot_general(table, prepared, (((1,), (1,)), ((), ())), preferred_element_type=F32)
        rows_ref[pl.ds(s, NBAND, stride=OWN_SEGS), :] = spectra
    length = NBAND * OWN_SEGS // len(outs)
    for n, out_ref in enumerate(outs):
        part = rows_ref[n * length : (n + 1) * length, :]
        out_ref[...] = part.astype(BF16).reshape(out_ref.shape)


def in_hbm(x):
    return pltpu.with_memory_space_constraint(x, pltpu.HBM)


def spectra(half, lead, count, name, chan, keep, pairs, records, tables):
    steps = np.arange(SEG, dtype=np.float64)
    taper = jnp.asarray((0.5 - 0.5 * np.cos(2.0 * math.pi * (steps + 0.5) / SEG)).astype(np.float32)[None])
    tail = (YX, 2 * BINS, OWN_SEGS, BLK)
    out = jax.ShapeDtypeStruct(lead + (OWN_BLKS,) + tail, BF16)
    out_spec = pl.BlockSpec(
        lead + (1,) + tail, lambda b, c, k, q: (0,) * len(lead) + (named(b, c, q)[0], 0, 0, 0, 0)
    )
    return pl.pallas_call(
        spectra_kernel,
        grid_spec=pltpu.PrefetchScalarGridSpec(
            num_scalar_prefetch=3,
            grid=(OWN_BLKS,),
            in_specs=[
                pl.BlockSpec((OWN_SEGS, BLK, SEG), lambda b, c, k, q: (0, named(b, c, q)[0], 0)),
                pl.BlockSpec((1, NBAND, SEG), lambda b, c, k, q: (c[0], half, 0)),
                pl.BlockSpec((1, SEG), lambda b, *_: (0, 0)),
            ],
            out_specs=[out_spec] * count,
            scratch_shapes=[pltpu.VMEM((NBAND * OWN_SEGS, BLK), F32)],
        ),
        out_shape=[out] * count,
        compiler_params=pltpu.CompilerParams(vmem_limit_bytes=16 * MIB),
        cost_estimate=pl.CostEstimate(flops=8192 * 256 * 256, bytes_accessed=11 * MIB, transcendentals=8192),
        name=name,
    )(chan, keep, pairs, in_hbm(records), in_hbm(tables), in_hbm(taper))


def whose(block, zl, core):
    return block // (CORE * OWN_BLKS) == zl, (block // OWN_BLKS) % CORE == core


def vmem():
    return pl.BlockSpec(memory_space=pltpu.VMEM)


def smem():
    return pl.BlockSpec(memory_space=pltpu.SMEM)


def hbm():
    return pl.BlockSpec(memory_space=pltpu.HBM)


def copy_either(first, one, two, to, sem):
    @pl.when(first)
    def _():
        pltpu.make_async_copy(one, to, sem).start()

    @pl.when(jnp.logical_not(first))
    def _():
        pltpu.make_async_copy(two, to, sem).start()


def rows_of(bin_):
    return pl.ds(bin_ * 2, 2)


def crossing(pairs, zl):
    flags = []
    alone, doubles = jnp.int32(0), jnp.int32(0)
    for p in range(NPAIR):
        a, b = (pairs[side, p] // (CORE * OWN_BLKS) == zl for side in range(2))
        one, both = jnp.where(a != b, 1, 0), jnp.where(a & b, 1, 0)
        flags.append((one, both))
        alone, doubles = alone + one, doubles + 2 * both
    moved = jnp.maximum(doubles - alone, 0) // 2
    inner, outer, seen = jnp.int32(0), jnp.int32(0), jnp.int32(0)
    plan = []
    for one, both in flags:
        at = inner
        inner = inner + one
        bins = []
        for _ in range(BINS):
            near = seen < moved
            bins.append((near, jnp.where(near, inner, outer)))
            inner = inner + jnp.where(near, both, 0)
            outer = outer + jnp.where(near, 0, both)
            seen = seen + both
        plan.append((one == 1, at, both == 1, bins))
    return inner, outer, plan


def couples_kernel(pairs_ref, out_ref):
    most = jnp.int32(LEAST)
    for zl in range(ZL):
        inner, outer, _ = crossing(pairs_ref, zl)
        most = jnp.maximum(most, jnp.maximum(inner, outer))
    out_ref[0] = most


def couples_of(pairs):
    return pl.pallas_call(
        couples_kernel,
        in_specs=[smem()],
        out_specs=smem(),
        out_shape=jax.ShapeDtypeStruct((1,), jnp.int32),
        name="couples",
    )(pairs)[0]


def sending_kernel(place_ref, pairs_ref, mine_ref, other_ref, inner_ref, outer_ref, sems):
    zl, core = place_ref[0], place_ref[1]
    plan = crossing(pairs_ref, zl)[2]

    def source(ref, block, bin_):
        return ref.at[block % OWN_BLKS, :, rows_of(bin_)]

    def move(block, bin_, to, sem):
        own = whose(block, zl, core)[1]
        copy_either(own, source(mine_ref, block, bin_), source(other_ref, block, bin_), to, sem)

    def await_all(p):
        for n in range(2 * BINS):
            pltpu.make_async_copy(source(mine_ref, 0, 0), inner_ref.at[0, 0], sems.at[p * BINS * 2 + n]).wait()

    for p in range(NPAIR):
        blocks = (pairs_ref[0, p], pairs_ref[1, p])
        one, at, both, bins = plan[p]

        @pl.when(one)
        def _(p=p, blocks=blocks, at=at):
            lone = jnp.where(whose(blocks[0], zl, core)[0], blocks[0], blocks[1])
            for bin_ in range(BINS):
                move(lone, bin_, inner_ref.at[at, bin_], sems.at[p * BINS * 2 + bin_])

        @pl.when(both)
        def _(p=p, blocks=blocks, bins=bins):
            for bin_ in range(BINS):
                near, slot = bins[bin_]
                for ref, chosen in ((inner_ref, near), (outer_ref, jnp.logical_not(near))):

                    @pl.when(chosen)
                    def _(bin_=bin_, slot=slot, ref=ref):
                        for side in range(2):
                            move(blocks[side], bin_, ref.at[slot, side], sems.at[(p * BINS + bin_) * 2 + side])

    for p in range(NPAIR):
        one, _, both, _ = plan[p]

        @pl.when(one)
        def _(p=p):
            for bin_ in range(BINS):
                sem = sems.at[p * BINS * 2 + bin_]
                pltpu.make_async_copy(source(mine_ref, 0, 0), inner_ref.at[0, 0], sem).wait()

        @pl.when(both)
        def _(p=p):
            await_all(p)


def sending(couples, place, pairs, mine, other):
    out = jax.ShapeDtypeStruct((couples, 2, YX, 2, OWN_SEGS, BLK), BF16)
    return pl.pallas_call(
        sending_kernel,
        in_specs=[smem(), smem(), hbm(), hbm()],
        out_specs=[hbm(), hbm()],
        out_shape=[out, out],
        scratch_shapes=[pltpu.SemaphoreType.DMA((NPAIR * BINS * 2,))],
        compiler_params=pltpu.CompilerParams(vmem_limit_bytes=4 * MIB),
        cost_estimate=pl.CostEstimate(flops=0, bytes_accessed=4 * MIB, transcendentals=0),
        name="sending",
    )(place, pairs, mine, other)


def kept_kernel(place_ref, pairs_ref, chip_ref, out_ref, sems):
    zl, core = place_ref[0], place_ref[1]
    for start in (True, False):
        for p in range(NPAIR):
            for side in range(2):
                block = pairs_ref[side, p]

                @pl.when(whose(block, zl, core)[0])
                def _(start=start, p=p, side=side, block=block):
                    source = chip_ref.at[block % (CORE * OWN_BLKS)]
                    copy = pltpu.make_async_copy(source, out_ref.at[:, p, side], sems.at[2 * p + side])
                    if start:
                        copy.start()
                    else:
                        copy.wait()


def came_kernel(place_ref, pairs_ref, inner_ref, outer_ref, kept_ref, out_ref, sems):
    zl, core = place_ref[0], place_ref[1]
    plan = crossing(pairs_ref, 1 - zl)[2]
    for start in (True, False):
        for p in range(NPAIR):
            one, at, both, bins = plan[p]
            away_a = jnp.logical_not(whose(pairs_ref[0, p], zl, core)[0])

            def go(side, bin_, near, one, two, p=p, start=start):
                to = out_ref.at[:, p, side, rows_of(bin_)]
                sem = sems.at[(2 * p + side) * BINS + bin_]
                if not start:
                    pltpu.make_async_copy(one, to, sem).wait()
                elif two is None:
                    pltpu.make_async_copy(one, to, sem).start()
                else:
                    copy_either(near, one, two, to, sem)

            for side, away in ((0, away_a), (1, jnp.logical_not(away_a))):

                @pl.when(one & away)
                def _(go=go, side=side, at=at):
                    for bin_ in range(BINS):
                        go(side, bin_, None, inner_ref.at[at, bin_], None)

            @pl.when(both)
            def _(go=go, bins=bins, start=start):
                for bin_ in range(BINS):
                    near, slot = bins[bin_]
                    slot = slot if start else 0
                    for side in range(2):
                        go(side, bin_, near, inner_ref.at[slot, side], outer_ref.at[slot, side])


def sides_of(kernel, name, place, pairs, *arrays):
    return pl.pallas_call(
        kernel,
        in_specs=[smem(), smem()] + [hbm()] * len(arrays),
        out_specs=hbm(),
        out_shape=jax.ShapeDtypeStruct((YX, NPAIR, 2, 2 * BINS, OWN_SEGS, BLK), BF16),
        scratch_shapes=[pltpu.SemaphoreType.DMA((2 * NPAIR * BINS,))],
        input_output_aliases={4: 0} if len(arrays) == 3 else {},
        compiler_params=pltpu.CompilerParams(vmem_limit_bytes=4 * MIB),
        cost_estimate=pl.CostEstimate(flops=0, bytes_accessed=3 * MIB, transcendentals=0),
        name=name,
    )(place, pairs, *arrays)


def products_kernel(factors_ref, out_ref, part_ref, rows_ref):
    length = YX * OWN_SEGS
    for p in range(NPAIR):
        for bin_ in range(BINS):
            x, y = (
                jnp.concatenate(
                    [factors_ref[:, p, side, 2 * bin_ + c].reshape(length, BLK) for c in range(2)], axis=1
                )
                for side in range(2)
            )
            g = lax.dot_general(x, y, (((0,), (0,)), ((), ())), preferred_element_type=F32)
            part_ref[0] = g[:BLK, :BLK] + g[BLK:, BLK:]
            part_ref[1] = g[BLK:, :BLK] - g[:BLK, BLK:]
            for c in range(2):
                for r in range(2):
                    at = p * 8 + r * 4 + bin_ * 2 + c
                    rows_ref[pl.ds(at, BLK // 2, stride=8 * NPAIR), :] = part_ref[c, pl.ds(r, BLK // 2, stride=2), :]
    out_ref[...] = rows_ref[...].astype(BF16)


def products(gathered):
    return pl.pallas_call(
        products_kernel,
        in_specs=[vmem()],
        out_specs=vmem(),
        out_shape=jax.ShapeDtypeStruct((BLK // 2 * NPAIR * 8, BLK), BF16),
        scratch_shapes=[pltpu.VMEM((2, BLK, BLK), F32), pltpu.VMEM((BLK // 2 * NPAIR * 8, BLK), F32)],
        compiler_params=pltpu.CompilerParams(vmem_limit_bytes=16 * MIB),
        cost_estimate=pl.CostEstimate(flops=2 * 8 * 256**3, bytes_accessed=3 * MIB, transcendentals=0),
        name="products",
    )(gathered)


def lags_kernel(scale, shares_ref, back_ref, out_ref, held_ref, sems):
    total = shares_ref[0].astype(F32)
    for z in range(1, ZH):
        total += shares_ref[z].astype(F32)
    stacked = total.astype(BF16)
    copies = []
    for r in range(2):
        lagged = lax.dot_general(stacked, back_ref[r], (((0,), (0,)), ((), ())), preferred_element_type=F32)
        rows = pl.ds(r * BLK, BLK)
        held_ref[rows, :] = lagged * scale
        copies.append(pltpu.make_async_copy(held_ref.at[rows], out_ref.at[0, rows], sems.at[r]))
        copies[-1].start()
    for copy in copies:
        copy.wait()


def backward():
    rows = inverse_rows()
    back = np.zeros((2, rows.shape[0], 2, 2 * BINS, NFFT), np.float32)
    for r in range(2):
        back[r, :, r] = rows
    return jnp.asarray(back.reshape(2, 4 * NBAND, NFFT), BF16)


def lags(shares, back, total):
    scale = 1.0 / math.sqrt(total * NBAND)
    return pl.pallas_call(
        lambda *refs: lags_kernel(scale, *refs),
        in_specs=[vmem(), vmem()],
        out_specs=hbm(),
        out_shape=pltpu.HBM((1, 2 * BLK, NFFT), F32),
        scratch_shapes=[pltpu.VMEM((2 * BLK, NFFT), F32), pltpu.SemaphoreType.DMA((2,))],
        compiler_params=pltpu.CompilerParams(vmem_limit_bytes=16 * MIB),
        cost_estimate=pl.CostEstimate(flops=4 * 512 * 128 * 512, bytes_accessed=2 * MIB, transcendentals=0),
        name="lags",
    )(shares, back)


def swap(x, axis):
    return lax.ppermute(x, axis, [(0, 1), (1, 0)])


def swap_outer(x):
    turns = []
    for zh in range(ZH):
        turns.append((zh * ZL, (zh - 1) % ZH * ZL + 1))
        turns.append((zh * ZL + 1, (zh + 1) % ZH * ZL))
    return lax.ppermute(x, ("zh", "zl"), turns)


def correlations(couples, place, pairs, chan, keep, records, tables, back, mine_far, other_far):
    inner, outer = sending(couples, place, pairs, mine_far, other_far)
    later, *_ = lax.optimization_barrier((chan, inner))
    inner, outer = swap(inner, "zl"), swap_outer(outer)
    (chip,) = spectra(0, (CORE,), 1, "spectra_near", later, keep, pairs, records, tables)
    chip = lax.all_to_all(chip, "core", 0, 0, tiled=True)
    chip = chip.reshape((CORE * OWN_BLKS,) + chip.shape[2:])
    kept = sides_of(kept_kernel, "kept", place, pairs, chip)
    sides = sides_of(came_kernel, "came", place, pairs, inner, outer, kept)
    gathered = lax.all_to_all(sides, ("y", "x"), 0, 0, tiled=True)
    shares = products(gathered).reshape(ZH * YX * NPAIR, 8, BLK)
    shares = lax.all_to_all(shares, ("zh", "y", "x", "zl", "core"), 0, 0, tiled=True)
    return lags(shares.reshape(ZH, YX * NPAIR * 8, BLK), back, records.shape[0] * ZH * YX)


def shards(records, keep, pairs):
    zl, core = lax.axis_index("zl"), lax.axis_index("core")
    place = jnp.stack([zl, core]).astype(jnp.int32)
    chan = (zl * CORE + core).astype(jnp.int32).reshape(1)
    sides_first = pairs.T
    tables = jnp.asarray(forward_tables(), BF16)
    mine_far, theirs_far = spectra(1, (), 2, "spectra_far", chan, keep, sides_first, records, tables)
    other_far = swap(theirs_far, "core")
    return lax.switch(
        couples_of(sides_first) - LEAST,
        [functools.partial(correlations, couples) for couples in range(LEAST, NPAIR + 1)],
        *(place, sides_first, chan, keep, records, tables, backward(), mine_far, other_far),
    )


def solution(mesh):
    fine = Mesh(mesh.devices.reshape(ZH, 4, 4, ZL, CORE), ("zh", "y", "x", "zl", "core"))
    win, chan = ("zh", "y", "x"), ("zl", "core")
    in_specs = (P(win, chan, None), P(win), P())
    out_specs = P(chan, win, None)
    return jax.shard_map(shards, mesh=fine, in_specs=in_specs, out_specs=out_specs, check_vma=False)
```

```python
import functools
import math

import jax
import jax.numpy as jnp
import numpy as np
from jax import lax
from jax.experimental import pallas as pl
from jax.experimental.pallas import tpu as pltpu
from jax.sharding import Mesh
from jax.sharding import PartitionSpec as P

BLK = 128
NBAND = 128
SEG = 256
NFFT = 512
NPAIR = 4
ZH, YX, ZL, CORE = 4, 16, 2, 2
OWN_SEGS = 16
OWN_BLKS = 4
BINS = 2
LEAST = 2
F32, BF16 = jnp.float32, jnp.bfloat16
MIB = 1 << 20


def bins_of(half, quarter):
    first = (half * ZL + quarter) * YX * BINS
    return (1 + first + np.arange(YX * BINS)).reshape(YX, BINS)


def forward_rows(bins):
    phase = (bins.reshape(-1, 1) * np.arange(SEG)[None, :]) % NFFT
    angle = phase.astype(np.float64) * (2.0 * math.pi / NFFT)
    both = np.stack([np.cos(angle), -np.sin(angle)], axis=1)
    return (both.reshape(-1, SEG) / math.sqrt(SEG)).astype(np.float32)


def forward_tables():
    tables = []
    for zl in range(ZL):
        for core in range(CORE):
            near = [bins_of(0, zl), bins_of(1, zl)]
            far = [bins_of(core, zl ^ 1), bins_of(core ^ 1, zl ^ 1)]
            tables.append(np.concatenate([forward_rows(bins) for bins in near + far]))
    return np.stack(tables)


def inverse_rows():
    order = np.stack(
        [np.stack([bins_of(core, zl) for core in range(CORE)], axis=1) for zl in range(ZL)], axis=1
    )
    phase = (order.reshape(-1, 1) * (np.arange(NFFT)[None, :] - NFFT // 2)) % NFFT
    angle = phase.astype(np.float64) * (2.0 * math.pi / NFFT)
    both = np.stack([np.cos(angle), -np.sin(angle)], axis=1)
    return both.reshape(-1, 2 * BINS, NFFT).astype(np.float32)


def named(step, chan_ref, pairs_ref):
    marks = []
    for k in range(OWN_BLKS):
        block = chan_ref[0] * OWN_BLKS + k
        mark = jnp.int32(0)
        for p in range(NPAIR):
            for side in range(2):
                mark = jnp.where(pairs_ref[side, p] == block, 1, mark)
        marks.append(mark)
    count = sum(marks[1:], marks[0])
    want = jnp.minimum(step, jnp.maximum(count - 1, 0))
    at, seen = jnp.int32(0), jnp.int32(0)
    for k, mark in enumerate(marks):
        at = jnp.where((mark == 1) & (seen == want), k, at)
        seen = seen + mark
    return at, step < count


def spectra_kernel(chan_ref, keep_ref, pairs_ref, *refs):
    there = named(pl.program_id(0), chan_ref, pairs_ref)[1]

    @pl.when(there)
    def _():
        block_spectra(keep_ref, *refs)


def block_spectra(keep_ref, records_ref, table_ref, taper_ref, *refs):
    outs, rows_ref = refs[:-1], refs[-1]
    table = table_ref[0]
    taper = taper_ref[...]
    for s in range(OWN_SEGS):
        samples = records_ref[s]
        centred = samples - jnp.mean(samples, axis=1, keepdims=True)
        power = jnp.mean(centred * centred, axis=1, keepdims=True)
        weight = keep_ref[s].astype(F32)
        prepared = (centred * (lax.rsqrt(power + 1e-06) * weight) * taper).astype(BF16)
        spectra = lax.dot_general(table, prepared, (((1,), (1,)), ((), ())), preferred_element_type=F32)
        rows_ref[pl.ds(s, NBAND, stride=OWN_SEGS), :] = spectra
    length = NBAND * OWN_SEGS // len(outs)
    for n, out_ref in enumerate(outs):
        part = rows_ref[n * length : (n + 1) * length, :]
        out_ref[...] = part.astype(BF16).reshape(out_ref.shape)


def in_hbm(x):
    return pltpu.with_memory_space_constraint(x, pltpu.HBM)


def spectra(half, lead, count, name, chan, keep, pairs, records, tables):
    steps = np.arange(SEG, dtype=np.float64)
    taper = jnp.asarray((0.5 - 0.5 * np.cos(2.0 * math.pi * (steps + 0.5) / SEG)).astype(np.float32)[None])
    tail = (YX, 2 * BINS, OWN_SEGS, BLK)
    out = jax.ShapeDtypeStruct(lead + (OWN_BLKS,) + tail, BF16)
    out_spec = pl.BlockSpec(
        lead + (1,) + tail, lambda b, c, k, q: (0,) * len(lead) + (named(b, c, q)[0], 0, 0, 0, 0)
    )
    return pl.pallas_call(
        spectra_kernel,
        grid_spec=pltpu.PrefetchScalarGridSpec(
            num_scalar_prefetch=3,
            grid=(OWN_BLKS,),
            in_specs=[
                pl.BlockSpec((OWN_SEGS, BLK, SEG), lambda b, c, k, q: (0, named(b, c, q)[0], 0)),
                pl.BlockSpec((1, NBAND, SEG), lambda b, c, k, q: (c[0], half, 0)),
                pl.BlockSpec((1, SEG), lambda b, *_: (0, 0)),
            ],
            out_specs=[out_spec] * count,
            scratch_shapes=[pltpu.VMEM((NBAND * OWN_SEGS, BLK), F32)],
        ),
        out_shape=[out] * count,
        compiler_params=pltpu.CompilerParams(vmem_limit_bytes=16 * MIB),
        cost_estimate=pl.CostEstimate(flops=8192 * 256 * 256, bytes_accessed=11 * MIB, transcendentals=8192),
        name=name,
    )(chan, keep, pairs, in_hbm(records), in_hbm(tables), in_hbm(taper))


def whose(block, zl, core):
    return block // (CORE * OWN_BLKS) == zl, (block // OWN_BLKS) % CORE == core


def vmem():
    return pl.BlockSpec(memory_space=pltpu.VMEM)


def smem():
    return pl.BlockSpec(memory_space=pltpu.SMEM)


def hbm():
    return pl.BlockSpec(memory_space=pltpu.HBM)


def copy_either(first, one, two, to, sem):
    @pl.when(first)
    def _():
        pltpu.make_async_copy(one, to, sem).start()

    @pl.when(jnp.logical_not(first))
    def _():
        pltpu.make_async_copy(two, to, sem).start()


def rows_of(bin_):
    return pl.ds(bin_ * 2, 2)


def crossing(pairs, zl):
    flags = []
    alone, doubles = jnp.int32(0), jnp.int32(0)
    for p in range(NPAIR):
        a, b = (pairs[side, p] // (CORE * OWN_BLKS) == zl for side in range(2))
        one, both = jnp.where(a != b, 1, 0), jnp.where(a & b, 1, 0)
        flags.append((one, both))
        alone, doubles = alone + one, doubles + 2 * both
    moved = jnp.maximum(doubles - alone, 0) // 2
    inner, outer, seen = jnp.int32(0), jnp.int32(0), jnp.int32(0)
    plan = []
    for one, both in flags:
        at = inner
        inner = inner + one
        bins = []
        for _ in range(BINS):
            near = seen < moved
            bins.append((near, jnp.where(near, inner, outer)))
            inner = inner + jnp.where(near, both, 0)
            outer = outer + jnp.where(near, 0, both)
            seen = seen + both
        plan.append((one == 1, at, both == 1, bins))
    return inner, outer, plan


def couples_kernel(pairs_ref, out_ref):
    most = jnp.int32(LEAST)
    for zl in range(ZL):
        inner, outer, _ = crossing(pairs_ref, zl)
        most = jnp.maximum(most, jnp.maximum(inner, outer))
    out_ref[0] = most


def couples_of(pairs):
    return pl.pallas_call(
        couples_kernel,
        in_specs=[smem()],
        out_specs=smem(),
        out_shape=jax.ShapeDtypeStruct((1,), jnp.int32),
        name="couples",
    )(pairs)[0]


def sending_kernel(place_ref, pairs_ref, mine_ref, other_ref, inner_ref, outer_ref, sems):
    zl, core = place_ref[0], place_ref[1]
    plan = crossing(pairs_ref, zl)[2]

    def source(ref, block, bin_):
        return ref.at[block % OWN_BLKS, :, rows_of(bin_)]

    def move(block, bin_, to, sem):
        own = whose(block, zl, core)[1]
        copy_either(own, source(mine_ref, block, bin_), source(other_ref, block, bin_), to, sem)

    def await_all(p):
        for n in range(2 * BINS):
            pltpu.make_async_copy(source(mine_ref, 0, 0), inner_ref.at[0, 0], sems.at[p * BINS * 2 + n]).wait()

    for p in range(NPAIR):
        blocks = (pairs_ref[0, p], pairs_ref[1, p])
        one, at, both, bins = plan[p]

        @pl.when(one)
        def _(p=p, blocks=blocks, at=at):
            lone = jnp.where(whose(blocks[0], zl, core)[0], blocks[0], blocks[1])
            for bin_ in range(BINS):
                move(lone, bin_, inner_ref.at[at, bin_], sems.at[p * BINS * 2 + bin_])

        @pl.when(both)
        def _(p=p, blocks=blocks, bins=bins):
            for bin_ in range(BINS):
                near, slot = bins[bin_]
                for ref, chosen in ((inner_ref, near), (outer_ref, jnp.logical_not(near))):

                    @pl.when(chosen)
                    def _(bin_=bin_, slot=slot, ref=ref):
                        for side in range(2):
                            move(blocks[side], bin_, ref.at[slot, side], sems.at[(p * BINS + bin_) * 2 + side])

    for p in range(NPAIR):
        one, _, both, _ = plan[p]

        @pl.when(one)
        def _(p=p):
            for bin_ in range(BINS):
                sem = sems.at[p * BINS * 2 + bin_]
                pltpu.make_async_copy(source(mine_ref, 0, 0), inner_ref.at[0, 0], sem).wait()

        @pl.when(both)
        def _(p=p):
            await_all(p)


def sending(couples, place, pairs, mine, other):
    out = jax.ShapeDtypeStruct((couples, 2, YX, 2, OWN_SEGS, BLK), BF16)
    return pl.pallas_call(
        sending_kernel,
        in_specs=[smem(), smem(), hbm(), hbm()],
        out_specs=[hbm(), hbm()],
        out_shape=[out, out],
        scratch_shapes=[pltpu.SemaphoreType.DMA((NPAIR * BINS * 2,))],
        compiler_params=pltpu.CompilerParams(vmem_limit_bytes=4 * MIB),
        cost_estimate=pl.CostEstimate(flops=0, bytes_accessed=4 * MIB, transcendentals=0),
        name="sending",
    )(place, pairs, mine, other)


def kept_kernel(place_ref, pairs_ref, chip_ref, out_ref, sems):
    zl, core = place_ref[0], place_ref[1]
    for start in (True, False):
        for p in range(NPAIR):
            for side in range(2):
                block = pairs_ref[side, p]

                @pl.when(whose(block, zl, core)[0])
                def _(start=start, p=p, side=side, block=block):
                    source = chip_ref.at[block % (CORE * OWN_BLKS)]
                    copy = pltpu.make_async_copy(source, out_ref.at[:, p, side], sems.at[2 * p + side])
                    if start:
                        copy.start()
                    else:
                        copy.wait()


def came_kernel(place_ref, pairs_ref, inner_ref, outer_ref, kept_ref, out_ref, sems):
    zl, core = place_ref[0], place_ref[1]
    plan = crossing(pairs_ref, 1 - zl)[2]
    for start in (True, False):
        for p in range(NPAIR):
            one, at, both, bins = plan[p]
            away_a = jnp.logical_not(whose(pairs_ref[0, p], zl, core)[0])

            def go(side, bin_, near, one, two, p=p, start=start):
                to = out_ref.at[:, p, side, rows_of(bin_)]
                sem = sems.at[(2 * p + side) * BINS + bin_]
                if not start:
                    pltpu.make_async_copy(one, to, sem).wait()
                elif two is None:
                    pltpu.make_async_copy(one, to, sem).start()
                else:
                    copy_either(near, one, two, to, sem)

            for side, away in ((0, away_a), (1, jnp.logical_not(away_a))):

                @pl.when(one & away)
                def _(go=go, side=side, at=at):
                    for bin_ in range(BINS):
                        go(side, bin_, None, inner_ref.at[at, bin_], None)

            @pl.when(both)
            def _(go=go, bins=bins, start=start):
                for bin_ in range(BINS):
                    near, slot = bins[bin_]
                    slot = slot if start else 0
                    for side in range(2):
                        go(side, bin_, near, inner_ref.at[slot, side], outer_ref.at[slot, side])


def sides_of(kernel, name, place, pairs, *arrays):
    return pl.pallas_call(
        kernel,
        in_specs=[smem(), smem()] + [hbm()] * len(arrays),
        out_specs=hbm(),
        out_shape=jax.ShapeDtypeStruct((YX, NPAIR, 2, 2 * BINS, OWN_SEGS, BLK), BF16),
        scratch_shapes=[pltpu.SemaphoreType.DMA((2 * NPAIR * BINS,))],
        input_output_aliases={4: 0} if len(arrays) == 3 else {},
        compiler_params=pltpu.CompilerParams(vmem_limit_bytes=4 * MIB),
        cost_estimate=pl.CostEstimate(flops=0, bytes_accessed=3 * MIB, transcendentals=0),
        name=name,
    )(place, pairs, *arrays)


def products_kernel(factors_ref, out_ref, part_ref, rows_ref):
    length = YX * OWN_SEGS
    for p in range(NPAIR):
        for bin_ in range(BINS):
            x, y = (
                jnp.concatenate(
                    [factors_ref[:, p, side, 2 * bin_ + c].reshape(length, BLK) for c in range(2)], axis=1
                )
                for side in range(2)
            )
            g = lax.dot_general(x, y, (((0,), (0,)), ((), ())), preferred_element_type=F32)
            part_ref[0] = g[:BLK, :BLK] + g[BLK:, BLK:]
            part_ref[1] = g[BLK:, :BLK] - g[:BLK, BLK:]
            for c in range(2):
                for r in range(2):
                    at = p * 8 + r * 4 + bin_ * 2 + c
                    rows_ref[pl.ds(at, BLK // 2, stride=8 * NPAIR), :] = part_ref[c, pl.ds(r, BLK // 2, stride=2), :]
    out_ref[...] = rows_ref[...].astype(BF16)


def products(gathered):
    return pl.pallas_call(
        products_kernel,
        in_specs=[vmem()],
        out_specs=vmem(),
        out_shape=jax.ShapeDtypeStruct((BLK // 2 * NPAIR * 8, BLK), BF16),
        scratch_shapes=[pltpu.VMEM((2, BLK, BLK), F32), pltpu.VMEM((BLK // 2 * NPAIR * 8, BLK), F32)],
        compiler_params=pltpu.CompilerParams(vmem_limit_bytes=16 * MIB),
        cost_estimate=pl.CostEstimate(flops=2 * 8 * 256**3, bytes_accessed=3 * MIB, transcendentals=0),
        name="products",
    )(gathered)


def lags_kernel(scale, shares_ref, back_ref, out_ref):
    total = shares_ref[0].astype(F32)
    for z in range(1, ZH):
        total += shares_ref[z].astype(F32)
    stacked = total.astype(BF16)
    lagged = lax.dot_general(stacked, back_ref[...], (((0,), (0,)), ((), ())), preferred_element_type=F32)
    for r in range(2):
        out_ref[0, r * BLK : (r + 1) * BLK, :] = lagged[:, r * NFFT : (r + 1) * NFFT] * scale


def backward():
    rows = inverse_rows()
    back = np.zeros((2, rows.shape[0], 2, 2 * BINS, NFFT), np.float32)
    for r in range(2):
        back[r, :, r] = rows
    back = back.reshape(2, 4 * NBAND, NFFT).transpose(1, 0, 2)
    return jnp.asarray(back.reshape(4 * NBAND, 2 * NFFT), BF16)


def lags(shares, back, total):
    scale = 1.0 / math.sqrt(total * NBAND)
    return pl.pallas_call(
        lambda *refs: lags_kernel(scale, *refs),
        in_specs=[vmem(), vmem()],
        out_specs=vmem(),
        out_shape=jax.ShapeDtypeStruct((1, 2 * BLK, NFFT), F32),
        compiler_params=pltpu.CompilerParams(vmem_limit_bytes=16 * MIB),
        cost_estimate=pl.CostEstimate(flops=4 * 512 * 128 * 512, bytes_accessed=2 * MIB, transcendentals=0),
        name="lags",
    )(shares, back)


def swap(x, axis):
    return lax.ppermute(x, axis, [(0, 1), (1, 0)])


def swap_outer(x):
    turns = []
    for zh in range(ZH):
        turns.append((zh * ZL, (zh - 1) % ZH * ZL + 1))
        turns.append((zh * ZL + 1, (zh + 1) % ZH * ZL))
    return lax.ppermute(x, ("zh", "zl"), turns)


def correlations(couples, place, pairs, chan, keep, records, tables, back, mine_far, other_far):
    inner, outer = sending(couples, place, pairs, mine_far, other_far)
    later, *_ = lax.optimization_barrier((chan, inner))
    inner, outer = swap(inner, "zl"), swap_outer(outer)
    (chip,) = spectra(0, (CORE,), 1, "spectra_near", later, keep, pairs, records, tables)
    chip = lax.all_to_all(chip, "core", 0, 0, tiled=True)
    chip = chip.reshape((CORE * OWN_BLKS,) + chip.shape[2:])
    kept = sides_of(kept_kernel, "kept", place, pairs, chip)
    sides = sides_of(came_kernel, "came", place, pairs, inner, outer, kept)
    gathered = lax.all_to_all(sides, ("y", "x"), 0, 0, tiled=True)
    shares = products(gathered).reshape(ZH * YX * NPAIR, 8, BLK)
    shares = lax.all_to_all(shares, ("zh", "y", "x", "zl", "core"), 0, 0, tiled=True)
    return lags(shares.reshape(ZH, YX * NPAIR * 8, BLK), back, records.shape[0] * ZH * YX)


def shards(records, keep, pairs):
    zl, core = lax.axis_index("zl"), lax.axis_index("core")
    place = jnp.stack([zl, core]).astype(jnp.int32)
    chan = (zl * CORE + core).astype(jnp.int32).reshape(1)
    sides_first = pairs.T
    tables = jnp.asarray(forward_tables(), BF16)
    mine_far, theirs_far = spectra(1, (), 2, "spectra_far", chan, keep, sides_first, records, tables)
    other_far = swap(theirs_far, "core")
    return lax.switch(
        couples_of(sides_first) - LEAST,
        [functools.partial(correlations, couples) for couples in range(LEAST, NPAIR + 1)],
        *(place, sides_first, chan, keep, records, tables, backward(), mine_far, other_far),
    )


def solution(mesh):
    fine = Mesh(mesh.devices.reshape(ZH, 4, 4, ZL, CORE), ("zh", "y", "x", "zl", "core"))
    win, chan = ("zh", "y", "x"), ("zl", "core")
    in_specs = (P(win, chan, None), P(win), P())
    out_specs = P(chan, win, None)
    return jax.shard_map(shards, mesh=fine, in_specs=in_specs, out_specs=out_specs, check_vma=False)
```
